512 devices in a mesh: dp: 8 (over y, core), proto: 64 (over x, z).
Axes of the slice: x: 4, y: 4, z: 16, core: 2. Of those that a mesh axis runs over, the one named last changes fastest.
Arguments:
- embeddings: bfloat16 [2048, 3, 256], P(('dp', 'proto')), may hold values from -3 to 3
- prototypes: bfloat16 [65536, 256], P('proto'), may hold values from -2 to 2
Outputs:
- embed_grad: float32 [2048, 3, 256], P(('dp', 'proto'))
- proto_grad: float32 [65536, 256], P('proto')
The draws below stay inside these ranges and needn't reach their ends.
All inputs are finite; a program needn't handle non-finite values.
Results may differ from the reference program's by a relative error of at most 0.0065.
Values may be sent and summed in bfloat16 or wider, within the bound.
No kernel may reach another device: no remote copies, remote signals or barrier semaphores. Data moves between devices by JAX's collectives and lax.ppermute only.
A program may use at most 64 MiB of HBM per device.

```python
import math
import jax
import jax.numpy as jnp
from jax import lax

D = 256
MODES = 3
ITERS = 3
KD = 1024
K = 65536
B = 2048


def shared_centers(key):
    group_count = max(4, K // 256)
    center_key = jax.random.fold_in(key, 101)
    return jax.random.truncated_normal(center_key, -3.0, 3.0, (group_count, D), jnp.float32) / math.sqrt(D)


def draw_prototypes(key, part):
    centers = shared_centers(key)
    key = jax.random.fold_in(key, 3)
    member_key, noise_key, scale_key = jax.random.split(key, 3)
    group_count = centers.shape[0]
    member = jax.random.randint(member_key, (K,), 0, group_count)
    noise = jax.random.truncated_normal(noise_key, -3.0, 3.0, (K, D), jnp.float32) / math.sqrt(D)
    pull = 0.6
    norms = jnp.exp(jax.random.uniform(scale_key, (K, 1), jnp.float32, math.log(0.7), math.log(1.4)))
    vectors = pull * centers[member] + math.sqrt(1.0 - pull * pull) * noise
    return (vectors * norms).astype(jnp.bfloat16)


def draw_embeddings(key, part):
    centers = shared_centers(key)
    key = jax.random.fold_in(key, 5)
    first_key, second_key, noise_key, scale_key = jax.random.split(key, 4)
    group_count = centers.shape[0]
    first = jax.random.randint(first_key, (B,), 0, group_count)
    second = jax.random.randint(second_key, (B,), 0, group_count)
    member = first * second // group_count
    noise = jax.random.truncated_normal(noise_key, -3.0, 3.0, (B, MODES, D), jnp.float32) / math.sqrt(D)
    pull = 0.6
    norms = jnp.exp(jax.random.uniform(scale_key, (B, MODES, 1), jnp.float32, math.log(0.7), math.log(1.4)))
    vectors = pull * centers[member][:, None, :] + math.sqrt(1.0 - pull * pull) * noise
    return (vectors * norms).astype(jnp.bfloat16)


def setup_inputs(seed: int = 0) -> dict:
    splits = jax.random.split(jax.random.key(seed), 3)
    embeddings = draw_embeddings(jax.random.fold_in(splits[2], 71), 0)
    prototypes = draw_prototypes(jax.random.fold_in(splits[2], 71), 0)
    return dict(embeddings=embeddings, prototypes=prototypes)


def reference(embeddings, prototypes):
    raw_rows = embeddings.astype(jnp.float32)
    row_scale = lax.rsqrt(lax.optimization_barrier(jnp.sum(raw_rows * raw_rows, axis=-1, keepdims=True)) + 1e-06)
    unit_rows = (raw_rows * row_scale).astype(jnp.bfloat16)
    flat_rows = unit_rows.reshape(B * MODES, D)
    line_count = B * MODES
    raw_protos = prototypes.astype(jnp.float32)
    proto_scale = lax.rsqrt(lax.optimization_barrier(jnp.sum(raw_protos * raw_protos, axis=-1, keepdims=True)) + 1e-06)
    unit_protos = (raw_protos * proto_scale).astype(jnp.bfloat16)
    proto_blocks = unit_protos.reshape(K // KD, KD, D)

    def scores_of(protos):
        return jnp.dot(flat_rows, protos.T, preferred_element_type=jnp.float32)

    def soft_step(carry, protos):
        return (carry + lax.optimization_barrier(jnp.sum(jnp.exp(scores_of(protos) * 10.0), axis=-1)), None)
    soft_total, _ = lax.scan(soft_step, jnp.zeros((line_count,), jnp.float32), proto_blocks)
    col_weight = jnp.ones((line_count,), jnp.float32)
    inverse_blocks = None
    for sweep_id in range(ITERS):

        def column_step(carry, protos, weights=col_weight):
            kernel = jnp.exp(scores_of(protos) * 20.0)
            mass = lax.optimization_barrier(jnp.sum((kernel * weights[:, None]).reshape(B, MODES, KD), axis=0))
            return (carry, 1.0 / mass)
        _, inverse_blocks = lax.scan(column_step, jnp.float32(0.0), proto_blocks)

        def row_step(carry, pair):
            protos, inverse = pair
            kernel = jnp.exp(scores_of(protos) * 20.0).reshape(B, MODES, KD)
            return (carry + lax.optimization_barrier(jnp.sum(kernel * inverse[None], axis=-1)).reshape(line_count), None)
        row_total, _ = lax.scan(row_step, jnp.zeros((line_count,), jnp.float32), (proto_blocks, inverse_blocks))
        col_weight = 1.0 / row_total
    coefficient = 64.0 * 10.0 / 6.0

    def grad_step(carry, pair):
        protos, inverse = pair
        scores = scores_of(protos)
        kernel = jnp.exp(scores * 20.0).reshape(B, MODES, KD)
        assigned = kernel * inverse[None] * col_weight.reshape(B, MODES, 1)
        predicted = jnp.exp(scores * 10.0).reshape(B, MODES, KD) / soft_total.reshape(B, MODES, 1)
        others = lax.optimization_barrier(jnp.sum(assigned, axis=1, keepdims=True)) - assigned
        logit_grad = (coefficient * (2.0 * predicted - others)).astype(jnp.bfloat16).reshape(line_count, KD)
        carry = carry + jnp.dot(logit_grad, protos, preferred_element_type=jnp.float32)
        proto_part = lax.dot_general(logit_grad, flat_rows, (((0,), (0,)), ((), ())), preferred_element_type=jnp.float32)
        return (carry, proto_part)
    unit_grad, proto_parts = lax.scan(grad_step, jnp.zeros((line_count, D), jnp.float32), (proto_blocks, inverse_blocks))
    unit_grad = unit_grad.reshape(B, MODES, D)
    inner = lax.optimization_barrier(jnp.sum(unit_grad * raw_rows, axis=-1, keepdims=True))
    embed_grad = row_scale * unit_grad - row_scale * row_scale * row_scale * inner * raw_rows
    proto_unit_grad = proto_parts.reshape(K, D)
    proto_inner = lax.optimization_barrier(jnp.sum(proto_unit_grad * raw_protos, axis=-1, keepdims=True))
    proto_grad = proto_scale * proto_unit_grad - proto_scale * proto_scale * proto_scale * proto_inner * raw_protos
    return (embed_grad, proto_grad)
```

```python
import functools

import jax
import jax.numpy as jnp
from jax import lax
from jax.experimental import pallas as pl
from jax.experimental.pallas import tpu as pltpu
from jax.sharding import Mesh, PartitionSpec as P

F32 = jnp.float32
BF16 = jnp.bfloat16
LANES = 128
COEFFICIENT = 64.0 * 10.0 / 6.0
NT = (((1,), (1,)), ((), ()))
SCALARS = pl.BlockSpec(memory_space=pltpu.SMEM)
WHOLE = pl.BlockSpec(memory_space=pltpu.VMEM)
ANYWHERE = pl.BlockSpec(memory_space=pl.ANY)


def call(body, name, out_shapes, in_specs, scratch=(), out_specs=None, aliases=None):
    many = isinstance(out_shapes, (list, tuple))
    return pl.pallas_call(
        body,
        name=name,
        in_specs=in_specs,
        out_shape=out_shapes,
        out_specs=out_specs or ([WHOLE] * len(out_shapes) if many else WHOLE),
        scratch_shapes=list(scratch),
        input_output_aliases=aliases or {},
        compiler_params=pltpu.CompilerParams(vmem_limit_bytes=28 * 1024 * 1024),
    )


def shape(dims, dtype):
    return jax.ShapeDtypeStruct(dims, dtype)


def tiles_to_line(block, first, count):
    return jnp.concatenate([block[first + j : first + j + 1] for j in range(count)], axis=1)


def line_to_tiles(ref, first, line):
    for j in range(line.shape[1] // LANES):
        ref[first + j : first + j + 1, :] = line[:, j * LANES : (j + 1) * LANES]


def tile_of(pair, tile):
    half = pair.shape[1] // LANES
    return pair[tile // half : tile // half + 1, (tile % half) * LANES : (tile % half + 1) * LANES]


def mode_of(pair, m, tiles):
    return jnp.concatenate([tile_of(pair, m * tiles + j) for j in range(tiles)], axis=1)


def lines_to_pair(lines):
    whole = jnp.concatenate(lines, axis=1)
    half = whole.shape[1] // 2
    return jnp.concatenate([whole[:, :half], whole[:, half:]], axis=0)


def upright(pair):
    count = 2 * pair.shape[1] // LANES
    block = jnp.concatenate([tile_of(pair, t) for t in range(count)] + [tile_of(pair, 0)] * (-count % 8), axis=0).T
    return jnp.concatenate([jnp.broadcast_to(block[:, t : t + 1], (LANES, LANES)) for t in range(count)], axis=0)


def two_terms(line):
    high = line.astype(BF16).astype(F32)
    row = lax.broadcasted_iota(jnp.int32, (16, line.shape[1]), 0)
    return jnp.where(row == 0, high, jnp.where(row == 1, line - high, 0.0)).astype(BF16)


def read_mode(ref, m, modes, owned):
    count = ref.shape[1] // (modes * owned)
    parts = [
        jnp.concatenate([ref[h, pl.ds(m * owned + i, count, stride=modes * owned), :] for h in range(ref.shape[0])], axis=1)
        for i in range(owned)
    ]
    return jnp.concatenate(parts, axis=0)


def score_body(modes, owned, rows_ref, protos_ref, kernel_ref, units_ref, unit_protos_ref, soft_ref, mass_ref, rows32):
    samples = rows_ref.shape[0] // modes
    width = protos_ref.shape[0]
    raw = protos_ref[...].astype(F32)
    scale = lax.rsqrt(jnp.sum(raw * raw, axis=-1, keepdims=True) + 1e-6)
    unit_protos_ref[...] = (raw * scale).astype(BF16)
    for h in range(rows32.shape[0]):
        rows32[h] = rows_ref[:, h * LANES : (h + 1) * LANES].astype(F32)
    lines = []
    for m in range(modes):
        rows = slice(m * samples, (m + 1) * samples)
        raw = read_mode(rows32, m, modes, owned)
        units = (raw * lax.rsqrt(jnp.sum(raw * raw, axis=-1, keepdims=True) + 1e-6)).astype(BF16)
        units_ref[rows, :] = units
        scores = lax.dot_general(units, unit_protos_ref[...], NT, preferred_element_type=F32)
        soft = jnp.exp(scores * 10.0)
        kernel = soft * soft
        kernel_ref[rows, :] = kernel.astype(BF16)
        line_to_tiles(mass_ref, m * (width // LANES), jnp.sum(kernel, axis=0, keepdims=True))
        folded = soft[:, :LANES]
        for j in range(1, width // LANES):
            folded = folded + soft[:, j * LANES : (j + 1) * LANES]
        high = folded.astype(BF16)
        low = (folded - high.astype(F32)).astype(BF16)
        ones = jnp.ones((16, LANES), BF16)
        line = lax.dot_general(ones, high, NT, preferred_element_type=F32)
        line = line + lax.dot_general(ones, low, NT, preferred_element_type=F32)
        lines.append(line[0:1])
    soft_ref[...] = lines_to_pair(lines)


def row_body(modes, mass_ref, kernel_ref, row_ref, inverse_ref):
    samples = kernel_ref.shape[0] // modes
    tiles = kernel_ref.shape[1] // LANES
    inverse = 1.0 / mass_ref[...]
    inverse_ref[...] = inverse
    lines = []
    for m in range(modes):
        terms = two_terms(tiles_to_line(inverse, m * tiles, tiles))
        kernel = kernel_ref[m * samples : (m + 1) * samples, :]
        line = lax.dot_general(terms, kernel, NT, preferred_element_type=F32)
        lines.append(line[0:1] + line[1:2])
    row_ref[...] = lines_to_pair(lines)


def column_body(modes, row_ref, kernel_ref, mass_ref):
    samples = kernel_ref.shape[0] // modes
    width = kernel_ref.shape[1]
    weight = 1.0 / row_ref[...]
    for m in range(modes):
        terms = two_terms(mode_of(weight, m, samples // LANES))
        kernel = kernel_ref[m * samples : (m + 1) * samples, :]
        line = jnp.dot(terms, kernel, preferred_element_type=F32)
        line_to_tiles(mass_ref, m * (width // LANES), line[0:1] + line[1:2])


def pull_body(modes, owned, place_ref, inverse_ref, units_ref, unit_protos_ref, *refs):
    pieces, grad32 = refs[:-1], refs[-1]
    samples = units_ref.shape[0] // modes
    width = unit_protos_ref.shape[0]
    tiles = width // LANES
    chunk = samples // owned // len(pieces)
    for m in range(modes):
        units = units_ref[m * samples : (m + 1) * samples, :]
        soft = jnp.exp(10.0 * lax.dot_general(units, unit_protos_ref[...], NT, preferred_element_type=F32))
        codes = soft * soft * tiles_to_line(inverse_ref[...], m * tiles, tiles)
        for part, value in enumerate((soft, codes)):
            first = (part * modes + m) * samples
            grad32[first : first + samples, :] = jnp.dot(
                value.astype(BF16), unit_protos_ref[...], preferred_element_type=F32
            )
    for step, piece in enumerate(pieces):
        place = lax.rem(place_ref[0] + step, len(pieces)) * chunk
        for j in range(2 * modes * owned):
            first = pl.multiple_of(place + j * (samples // owned), chunk)
            piece[j * chunk : (j + 1) * chunk, :] = grad32[pl.ds(first, chunk), :].astype(BF16)


def combine_body(modes, owned, place_ref, totals_ref, tied_ref, *refs):
    pieces, (rows_ref, weights, unit) = refs[:-3], refs[-3:]
    total = functools.reduce(jnp.add, [piece[...].astype(F32) for piece in pieces])
    height = total.shape[0] // 2
    chunk = height // (modes * owned)
    weights[0] = upright(COEFFICIENT / totals_ref[0:2])
    weights[1] = upright(2.0 * COEFFICIENT / totals_ref[2:4])
    samples = weights.shape[1] // modes

    def weighted(kind, first, m):
        factor = jnp.concatenate(
            [
                weights[kind, pl.ds(pl.multiple_of(m * samples + (i * len(pieces) + place_ref[0]) * chunk, chunk), chunk), :]
                for i in range(owned)
            ],
            axis=0,
        )
        block = total[first + m * owned * chunk : first + (m + 1) * owned * chunk]
        return block * jnp.concatenate([factor] * (block.shape[1] // LANES), axis=1)

    codes = [weighted(0, height, m) for m in range(modes)]
    for m in range(modes):
        others = [codes[n] for n in range(modes) if n != m]
        grad = weighted(1, 0, m) - functools.reduce(jnp.add, others)
        for h in range(unit.shape[0]):
            unit[h, m * owned * chunk : (m + 1) * owned * chunk, :] = grad[:, h * LANES : (h + 1) * LANES]
    for j in range(rows_ref.shape[0]):
        rows_ref[j] = jnp.concatenate(
            [unit[h, pl.ds(j, modes * owned, stride=chunk), :] for h in range(unit.shape[0])], axis=1
        ).astype(BF16)


def proto_body(modes, totals_ref, inverse_ref, units_ref, unit_protos_ref, *refs):
    proto_ref = refs[-1]
    samples = units_ref.shape[0] // modes
    width = unit_protos_ref.shape[0]
    tiles = width // LANES
    inverse = inverse_ref[...].T
    weight = COEFFICIENT / totals_ref[0:2]
    spread = 2.0 * COEFFICIENT / totals_ref[2:4]
    weight = [mode_of(weight, m, samples // LANES) for m in range(modes)]
    spread = [mode_of(spread, m, samples // LANES) for m in range(modes)]
    step = 256
    for k in range(0, width, step):
        scores = lax.dot_general(unit_protos_ref[k : k + step, :], units_ref[...], NT, preferred_element_type=F32)
        codes, predicted = [], []
        for m in range(modes):
            first = m * tiles + k // LANES
            upright_inverse = jnp.concatenate([inverse[:, first + j : first + j + 1] for j in range(step // LANES)], axis=0)
            soft = jnp.exp(10.0 * scores[:, m * samples : (m + 1) * samples])
            codes.append(soft * soft * upright_inverse * weight[m])
            predicted.append(soft * spread[m])
        logit = [
            (predicted[m] - functools.reduce(jnp.add, [codes[n] for n in range(modes) if n != m])).astype(BF16)
            for m in range(modes)
        ]
        proto_ref[k : k + step, :] = jnp.dot(
            jnp.concatenate(logit, axis=1), units_ref[...], preferred_element_type=F32
        ).astype(BF16)


def middle_body(place_ref, parts_ref, protos_ref, tied_ref, grad_ref, tied_out_ref):
    total = jnp.sum(parts_ref[...].astype(F32), axis=0)
    share = total.shape[0]
    raw = protos_ref[pl.ds(pl.multiple_of(place_ref[0] * share, share), share), :].astype(F32)
    scale = lax.rsqrt(jnp.sum(raw * raw, axis=-1, keepdims=True) + 1e-6)
    inner = jnp.sum(total * raw, axis=-1, keepdims=True)
    grad_ref[...] = (scale * total - scale * scale * scale * inner * raw).astype(BF16)


def last_body(parts_ref, raw_ref, grad_ref):
    total = jnp.sum(parts_ref[...].astype(F32), axis=0)
    raw = raw_ref[...].astype(F32)
    scale = lax.rsqrt(jnp.sum(raw * raw, axis=-1, keepdims=True) + 1e-6)
    inner = jnp.sum(total * raw, axis=-1, keepdims=True)
    grad = scale * total - scale * scale * scale * inner * raw
    modes, owned = grad_ref.shape[:2]
    for m in range(modes):
        grad_ref[m] = grad[m * owned : (m + 1) * owned]


def exchange(x, axes):
    return lax.all_to_all(x, axes, 0, 0, tiled=True)


def copies(x, axes, count):
    return exchange(jnp.broadcast_to(x[None], (count,) + x.shape), axes)


def gather(x, axes, count):
    return copies(x, axes, count).reshape((count * x.shape[0],) + x.shape[1:])


def sum_over(x, axes, count):
    return jnp.sum(copies(x.astype(BF16), axes, count).astype(F32), axis=0)


def shift(x, axis, count, step):
    return lax.ppermute(x, axis, [(i, (i + step) % count) for i in range(count)]) if step else x


def per_device(sizes, embeddings, prototypes):
    modes, width = embeddings.shape[1:]
    own_samples = embeddings.shape[0]
    owned = own_samples * modes
    local_protos = prototypes.shape[0]
    ny, nc, nx, nz = (sizes[a] for a in ("y", "core", "x", "z"))
    dp = ("y", "core")
    groups = ny * nc
    lines = owned * nx * nz
    x_lines = lines // nx
    mass_shape = shape((modes * local_protos // LANES, LANES), F32)
    row_shape = shape((2, lines // 2), F32)
    units_shape = shape((lines, width), BF16)
    dp_place = lax.axis_index(dp).reshape(1)
    x_place = lax.axis_index("x").reshape(1)

    row_call = call(functools.partial(row_body, modes), "row_sum", [row_shape, mass_shape], [WHOLE] * 2)
    column_call = call(functools.partial(column_body, modes), "column_sum", mass_shape, [WHOLE] * 2)

    raw_rows = embeddings.transpose(1, 0, 2).reshape(owned, width)
    gathered = gather(gather(raw_rows, "z", nz), "x", nx)
    kernel, units, unit_protos, soft, mass = call(
        functools.partial(score_body, modes, own_samples),
        "scores",
        [shape((lines, local_protos), BF16), units_shape, shape((local_protos, width), BF16), row_shape, mass_shape],
        [WHOLE] * 2,
        [pltpu.VMEM((width // LANES, lines, LANES), F32)],
    )(gathered, prototypes)

    for _ in range(2):
        row, _ = row_call(sum_over(mass, dp, groups), kernel)
        mass = column_call(sum_over(row, ("x", "z"), nx * nz), kernel)
    row, inverse = row_call(sum_over(mass, dp, groups), kernel)
    pieces = call(
        functools.partial(pull_body, modes, own_samples),
        "pull",
        [shape((2 * x_lines, width), BF16)] * nx,
        [SCALARS] + [WHOLE] * 3,
        [pltpu.VMEM((2 * lines, width), F32)],
    )(x_place, inverse, units, unit_protos)
    pieces = [shift(piece, "x", nx, step) for step, piece in enumerate(pieces)]
    totals = sum_over(jnp.concatenate([row, soft], axis=0), ("x", "z"), nx * nz)

    proto_part = call(
        functools.partial(proto_body, modes), "proto_part", shape((local_protos, width), BF16), [WHOLE] * 4 + [ANYWHERE] * nx
    )(totals, inverse, units, unit_protos, *pieces)
    rows = call(
        functools.partial(combine_body, modes, own_samples),
        "combine",
        shape((nz, owned, width), BF16),
        [SCALARS, WHOLE, ANYWHERE] + [WHOLE] * nx,
        [pltpu.VMEM((2, lines, LANES), F32), pltpu.VMEM((width // LANES, x_lines, LANES), F32)],
    )(x_place, totals, proto_part, *pieces)
    proto_part = exchange(proto_part, dp).reshape(groups, local_protos // groups, width)
    proto_grad, rows = call(
        middle_body,
        "middle",
        [shape((local_protos // groups, width), BF16), shape(rows.shape, BF16)],
        [SCALARS, WHOLE, WHOLE, ANYWHERE],
        (),
        [WHOLE, ANYWHERE],
        {3: 1},
    )(dp_place, proto_part, prototypes, rows)
    rows = exchange(rows, "z")
    proto_grad = lax.all_gather(proto_grad, dp, axis=0, tiled=True).astype(F32)
    embed_grad = call(last_body, "last", shape((modes, own_samples, width), F32), [WHOLE] * 2)(rows, raw_rows)
    return (embed_grad.transpose(1, 0, 2), proto_grad)


def solution(mesh):
    sizes = dict(y=mesh.shape["dp"] // 2, core=2, x=4, z=mesh.shape["proto"] // 4)
    fine = Mesh(mesh.devices.reshape(tuple(sizes.values())), tuple(sizes))
    specs = (P(("y", "core", "x", "z"), None, None), P(("x", "z"), None))
    return jax.shard_map(
        functools.partial(per_device, sizes), mesh=fine, in_specs=specs, out_specs=specs, check_vma=False
    )
```

```python
import functools

import jax
import jax.numpy as jnp
from jax import lax
from jax.experimental import pallas as pl
from jax.experimental.pallas import tpu as pltpu
from jax.sharding import Mesh, PartitionSpec as P

F32 = jnp.float32
BF16 = jnp.bfloat16
LANES = 128
COEFFICIENT = 64.0 * 10.0 / 6.0
NT = (((1,), (1,)), ((), ()))
SCALARS = pl.BlockSpec(memory_space=pltpu.SMEM)
WHOLE = pl.BlockSpec(memory_space=pltpu.VMEM)
ANYWHERE = pl.BlockSpec(memory_space=pl.ANY)


def call(body, name, out_shapes, in_specs, scratch=(), out_specs=None, aliases=None):
    many = isinstance(out_shapes, (list, tuple))
    return pl.pallas_call(
        body,
        name=name,
        in_specs=in_specs,
        out_shape=out_shapes,
        out_specs=out_specs or ([WHOLE] * len(out_shapes) if many else WHOLE),
        scratch_shapes=list(scratch),
        input_output_aliases=aliases or {},
        compiler_params=pltpu.CompilerParams(vmem_limit_bytes=28 * 1024 * 1024),
    )


def shape(dims, dtype):
    return jax.ShapeDtypeStruct(dims, dtype)


def tiles_to_line(block, first, count):
    return jnp.concatenate([block[first + j : first + j + 1] for j in range(count)], axis=1)


def line_to_tiles(ref, first, line):
    for j in range(line.shape[1] // LANES):
        ref[first + j : first + j + 1, :] = line[:, j * LANES : (j + 1) * LANES]


def tile_of(pair, tile):
    half = pair.shape[1] // LANES
    return pair[tile // half : tile // half + 1, (tile % half) * LANES : (tile % half + 1) * LANES]


def mode_of(pair, m, tiles):
    return jnp.concatenate([tile_of(pair, m * tiles + j) for j in range(tiles)], axis=1)


def lines_to_pair(lines):
    whole = jnp.concatenate(lines, axis=1)
    half = whole.shape[1] // 2
    return jnp.concatenate([whole[:, :half], whole[:, half:]], axis=0)


def upright(pair):
    count = 2 * pair.shape[1] // LANES
    block = jnp.concatenate([tile_of(pair, t) for t in range(count)] + [tile_of(pair, 0)] * (-count % 8), axis=0).T
    return jnp.concatenate([jnp.broadcast_to(block[:, t : t + 1], (LANES, LANES)) for t in range(count)], axis=0)


def two_terms(line):
    high = line.astype(BF16).astype(F32)
    row = lax.broadcasted_iota(jnp.int32, (16, line.shape[1]), 0)
    return jnp.where(row == 0, high, jnp.where(row == 1, line - high, 0.0)).astype(BF16)


def read_mode(ref, m, modes, owned, halves):
    per_owner = halves * modes * owned
    count = ref.shape[0] // per_owner
    parts = [
        jnp.concatenate(
            [ref[pl.ds((h * modes + m) * owned + i, count, stride=per_owner), :] for h in range(halves)], axis=1
        )
        for i in range(owned)
    ]
    return jnp.concatenate(parts, axis=0)


def score_body(modes, owned, rows_ref, protos_ref, kernel_ref, units_ref, unit_protos_ref, soft_ref, mass_ref, rows32):
    samples = units_ref.shape[0] // modes
    width = protos_ref.shape[0]
    halves = protos_ref.shape[1] // LANES
    raw = protos_ref[...].astype(F32)
    scale = lax.rsqrt(jnp.sum(raw * raw, axis=-1, keepdims=True) + 1e-6)
    unit_protos_ref[...] = (raw * scale).astype(BF16)
    rows32[...] = rows_ref[...].astype(F32)
    lines = []
    for m in range(modes):
        rows = slice(m * samples, (m + 1) * samples)
        raw = read_mode(rows32, m, modes, owned, halves)
        units = (raw * lax.rsqrt(jnp.sum(raw * raw, axis=-1, keepdims=True) + 1e-6)).astype(BF16)
        units_ref[rows, :] = units
        scores = lax.dot_general(units, unit_protos_ref[...], NT, preferred_element_type=F32)
        soft = jnp.exp(scores * 10.0)
        kernel = soft * soft
        kernel_ref[rows, :] = kernel.astype(BF16)
        line_to_tiles(mass_ref, m * (width // LANES), jnp.sum(kernel, axis=0, keepdims=True))
        folded = soft[:, :LANES]
        for j in range(1, width // LANES):
            folded = folded + soft[:, j * LANES : (j + 1) * LANES]
        high = folded.astype(BF16)
        low = (folded - high.astype(F32)).astype(BF16)
        ones = jnp.ones((16, LANES), BF16)
        line = lax.dot_general(ones, high, NT, preferred_element_type=F32)
        line = line + lax.dot_general(ones, low, NT, preferred_element_type=F32)
        lines.append(line[0:1])
    soft_ref[...] = lines_to_pair(lines)


def row_body(modes, mass_ref, kernel_ref, row_ref, inverse_ref):
    samples = kernel_ref.shape[0] // modes
    tiles = kernel_ref.shape[1] // LANES
    inverse = 1.0 / mass_ref[...]
    inverse_ref[...] = inverse
    lines = []
    for m in range(modes):
        terms = two_terms(tiles_to_line(inverse, m * tiles, tiles))
        kernel = kernel_ref[m * samples : (m + 1) * samples, :]
        line = lax.dot_general(terms, kernel, NT, preferred_element_type=F32)
        lines.append(line[0:1] + line[1:2])
    row_ref[...] = lines_to_pair(lines)


def column_body(modes, row_ref, kernel_ref, mass_ref):
    samples = kernel_ref.shape[0] // modes
    width = kernel_ref.shape[1]
    weight = 1.0 / row_ref[...]
    for m in range(modes):
        terms = two_terms(mode_of(weight, m, samples // LANES))
        kernel = kernel_ref[m * samples : (m + 1) * samples, :]
        line = jnp.dot(terms, kernel, preferred_element_type=F32)
        line_to_tiles(mass_ref, m * (width // LANES), line[0:1] + line[1:2])


def pull_body(modes, owned, place_ref, inverse_ref, units_ref, unit_protos_ref, *refs):
    pieces, grad32 = refs[:-1], refs[-1]
    samples = units_ref.shape[0] // modes
    width = unit_protos_ref.shape[0]
    tiles = width // LANES
    chunk = samples // owned // len(pieces)
    for m in range(modes):
        units = units_ref[m * samples : (m + 1) * samples, :]
        soft = jnp.exp(10.0 * lax.dot_general(units, unit_protos_ref[...], NT, preferred_element_type=F32))
        codes = soft * soft * tiles_to_line(inverse_ref[...], m * tiles, tiles)
        for part, value in enumerate((soft, codes)):
            first = (part * modes + m) * samples
            grad32[first : first + samples, :] = jnp.dot(
                value.astype(BF16), unit_protos_ref[...], preferred_element_type=F32
            )
    for step, piece in enumerate(pieces):
        place = lax.bitwise_xor(place_ref[0], jnp.int32(step)) * chunk
        for j in range(2 * modes * owned):
            first = pl.multiple_of(place + j * (samples // owned), chunk)
            piece[j * chunk : (j + 1) * chunk, :] = grad32[pl.ds(first, chunk), :].astype(BF16)


def combine_body(modes, owned, place_ref, totals_ref, tied_ref, *refs):
    pieces, (rows_ref, weights, unit) = refs[:-3], refs[-3:]
    total = functools.reduce(jnp.add, [piece[...].astype(F32) for piece in pieces])
    height = total.shape[0] // 2
    chunk = height // (modes * owned)
    weights[0] = upright(COEFFICIENT / totals_ref[0:2])
    weights[1] = upright(2.0 * COEFFICIENT / totals_ref[2:4])
    samples = weights.shape[1] // modes

    def weighted(kind, first, m):
        factor = jnp.concatenate(
            [
                weights[kind, pl.ds(pl.multiple_of(m * samples + (i * len(pieces) + place_ref[0]) * chunk, chunk), chunk), :]
                for i in range(owned)
            ],
            axis=0,
        )
        block = total[first + m * owned * chunk : first + (m + 1) * owned * chunk]
        return block * jnp.concatenate([factor] * (block.shape[1] // LANES), axis=1)

    codes = [weighted(0, height, m) for m in range(modes)]
    for m in range(modes):
        others = [codes[n] for n in range(modes) if n != m]
        grad = weighted(1, 0, m) - functools.reduce(jnp.add, others)
        for h in range(unit.shape[0]):
            unit[h, m * owned * chunk : (m + 1) * owned * chunk, :] = grad[:, h * LANES : (h + 1) * LANES]
    for j in range(rows_ref.shape[0]):
        rows_ref[j] = jnp.concatenate(
            [unit[h, pl.ds(j, modes * owned, stride=chunk), :] for h in range(unit.shape[0])], axis=0
        ).astype(BF16)


def proto_body(modes, totals_ref, inverse_ref, units_ref, unit_protos_ref, *refs):
    proto_ref = refs[-1]
    samples = units_ref.shape[0] // modes
    width = unit_protos_ref.shape[0]
    tiles = width // LANES
    inverse = inverse_ref[...].T
    weight = COEFFICIENT / totals_ref[0:2]
    spread = 2.0 * COEFFICIENT / totals_ref[2:4]
    weight = [mode_of(weight, m, samples // LANES) for m in range(modes)]
    spread = [mode_of(spread, m, samples // LANES) for m in range(modes)]
    step = 256
    for k in range(0, width, step):
        scores = lax.dot_general(unit_protos_ref[k : k + step, :], units_ref[...], NT, preferred_element_type=F32)
        codes, predicted = [], []
        for m in range(modes):
            first = m * tiles + k // LANES
            upright_inverse = jnp.concatenate([inverse[:, first + j : first + j + 1] for j in range(step // LANES)], axis=0)
            soft = jnp.exp(10.0 * scores[:, m * samples : (m + 1) * samples])
            codes.append(soft * soft * upright_inverse * weight[m])
            predicted.append(soft * spread[m])
        logit = [
            (predicted[m] - functools.reduce(jnp.add, [codes[n] for n in range(modes) if n != m])).astype(BF16)
            for m in range(modes)
        ]
        proto_ref[k : k + step, :] = jnp.dot(
            jnp.concatenate(logit, axis=1), units_ref[...], preferred_element_type=F32
        ).astype(BF16)


def middle_body(place_ref, parts_ref, protos_ref, tied_ref, grad_ref, tied_out_ref):
    total = jnp.sum(parts_ref[...].astype(F32), axis=0)
    share = total.shape[0]
    raw = protos_ref[pl.ds(pl.multiple_of(place_ref[0] * share, share), share), :].astype(F32)
    scale = lax.rsqrt(jnp.sum(raw * raw, axis=-1, keepdims=True) + 1e-6)
    inner = jnp.sum(total * raw, axis=-1, keepdims=True)
    grad_ref[...] = (scale * total - scale * scale * scale * inner * raw).astype(BF16)


def last_body(parts_ref, raw_ref, grad_ref):
    total = jnp.sum(parts_ref[...].astype(F32), axis=0)
    raw = raw_ref[...].astype(F32)
    count = raw.shape[0]
    total = jnp.concatenate([total[h : h + count] for h in range(0, total.shape[0], count)], axis=1)
    scale = lax.rsqrt(jnp.sum(raw * raw, axis=-1, keepdims=True) + 1e-6)
    inner = jnp.sum(total * raw, axis=-1, keepdims=True)
    grad = scale * total - scale * scale * scale * inner * raw
    modes, owned = grad_ref.shape[:2]
    for m in range(modes):
        grad_ref[m] = grad[m * owned : (m + 1) * owned]


def exchange(x, axes):
    return lax.all_to_all(x, axes, 0, 0, tiled=True)


def copies(x, axes, count):
    return exchange(jnp.broadcast_to(x[None], (count,) + x.shape), axes)


def gather(x, axes, count):
    return copies(x, axes, count).reshape((count * x.shape[0],) + x.shape[1:])


def sum_over(x, axes, count):
    return jnp.sum(copies(x.astype(BF16), axes, count).astype(F32), axis=0)


def swap(x, axis, count, step):
    return lax.ppermute(x, axis, [(i, i ^ step) for i in range(count)]) if step else x


def per_device(sizes, embeddings, prototypes):
    modes, width = embeddings.shape[1:]
    own_samples = embeddings.shape[0]
    owned = own_samples * modes
    local_protos = prototypes.shape[0]
    ny, nc, nx, nz = (sizes[a] for a in ("y", "core", "x", "z"))
    dp = ("y", "core")
    groups = ny * nc
    lines = owned * nx * nz
    x_lines = lines // nx
    mass_shape = shape((modes * local_protos // LANES, LANES), F32)
    row_shape = shape((2, lines // 2), F32)
    units_shape = shape((lines, width), BF16)
    dp_place = lax.axis_index(dp).reshape(1)
    x_place = lax.axis_index("x").reshape(1)

    row_call = call(functools.partial(row_body, modes), "row_sum", [row_shape, mass_shape], [WHOLE] * 2)
    column_call = call(functools.partial(column_body, modes), "column_sum", mass_shape, [WHOLE] * 2)

    raw_rows = embeddings.transpose(1, 0, 2).reshape(owned, width)
    raw_tiles = jnp.concatenate([raw_rows[:, h : h + LANES] for h in range(0, width, LANES)], axis=0)
    gathered = gather(gather(raw_tiles, "z", nz), "x", nx)
    kernel, units, unit_protos, soft, mass = call(
        functools.partial(score_body, modes, own_samples),
        "scores",
        [shape((lines, local_protos), BF16), units_shape, shape((local_protos, width), BF16), row_shape, mass_shape],
        [WHOLE] * 2,
        [pltpu.VMEM(gathered.shape, F32)],
    )(gathered, prototypes)

    for _ in range(2):
        row, _ = row_call(sum_over(mass, dp, groups), kernel)
        mass = column_call(sum_over(row, ("x", "z"), nx * nz), kernel)
    row, inverse = row_call(sum_over(mass, dp, groups), kernel)
    pieces = call(
        functools.partial(pull_body, modes, own_samples),
        "pull",
        [shape((2 * x_lines, width), BF16)] * nx,
        [SCALARS] + [WHOLE] * 3,
        [pltpu.VMEM((2 * lines, width), F32)],
    )(x_place, inverse, units, unit_protos)
    pieces = [swap(piece, "x", nx, step) for step, piece in enumerate(pieces)]
    totals = sum_over(jnp.concatenate([row, soft], axis=0), ("x", "z"), nx * nz)

    proto_part = call(
        functools.partial(proto_body, modes), "proto_part", shape((local_protos, width), BF16), [WHOLE] * 4 + [ANYWHERE] * nx
    )(totals, inverse, units, unit_protos, *pieces)
    rows = call(
        functools.partial(combine_body, modes, own_samples),
        "combine",
        shape((nz, owned * width // LANES, LANES), BF16),
        [SCALARS, WHOLE, ANYWHERE] + [WHOLE] * nx,
        [pltpu.VMEM((2, lines, LANES), F32), pltpu.VMEM((width // LANES, x_lines, LANES), F32)],
    )(x_place, totals, proto_part, *pieces)
    proto_part = exchange(proto_part, dp).reshape(groups, local_protos // groups, width)
    proto_grad, rows = call(
        middle_body,
        "middle",
        [shape((local_protos // groups, width), BF16), shape(rows.shape, BF16)],
        [SCALARS, WHOLE, WHOLE, ANYWHERE],
        (),
        [WHOLE, ANYWHERE],
        {3: 1},
    )(dp_place, proto_part, prototypes, rows)
    rows = exchange(rows, "z")
    proto_grad = lax.all_gather(proto_grad, dp, axis=0, tiled=True).astype(F32)
    embed_grad = call(last_body, "last", shape((modes, own_samples, width), F32), [WHOLE] * 2)(rows, raw_rows)
    return (embed_grad.transpose(1, 0, 2), proto_grad)


def solution(mesh):
    sizes = dict(y=mesh.shape["dp"] // 2, core=2, x=4, z=mesh.shape["proto"] // 4)
    fine = Mesh(mesh.devices.reshape(tuple(sizes.values())), tuple(sizes))
    specs = (P(("y", "core", "x", "z"), None, None), P(("x", "z"), None))
    return jax.shard_map(
        functools.partial(per_device, sizes), mesh=fine, in_specs=specs, out_specs=specs, check_vma=False
    )
```

```python
import functools

import jax
import jax.numpy as jnp
from jax import lax
from jax.experimental import pallas as pl
from jax.experimental.pallas import tpu as pltpu
from jax.sharding import Mesh, PartitionSpec as P

F32 = jnp.float32
BF16 = jnp.bfloat16
LANES = 128
COEFFICIENT = 64.0 * 10.0 / 6.0
NT = (((1,), (1,)), ((), ()))
SCALARS = pl.BlockSpec(memory_space=pltpu.SMEM)
WHOLE = pl.BlockSpec(memory_space=pltpu.VMEM)
ANYWHERE = pl.BlockSpec(memory_space=pl.ANY)


def call(body, name, out_shapes, in_specs, scratch=(), out_specs=None, aliases=None):
    many = isinstance(out_shapes, (list, tuple))
    return pl.pallas_call(
        body,
        name=name,
        in_specs=in_specs,
        out_shape=out_shapes,
        out_specs=out_specs or ([WHOLE] * len(out_shapes) if many else WHOLE),
        scratch_shapes=list(scratch),
        input_output_aliases=aliases or {},
        compiler_params=pltpu.CompilerParams(vmem_limit_bytes=28 * 1024 * 1024),
    )


def shape(dims, dtype):
    return jax.ShapeDtypeStruct(dims, dtype)


def tiles_to_line(block, first, count):
    return jnp.concatenate([block[first + j : first + j + 1] for j in range(count)], axis=1)


def line_to_tiles(ref, first, line):
    for j in range(line.shape[1] // LANES):
        ref[first + j : first + j + 1, :] = line[:, j * LANES : (j + 1) * LANES]


def tile_of(pair, tile):
    half = pair.shape[1] // LANES
    return pair[tile // half : tile // half + 1, (tile % half) * LANES : (tile % half + 1) * LANES]


def mode_of(pair, m, tiles):
    return jnp.concatenate([tile_of(pair, m * tiles + j) for j in range(tiles)], axis=1)


def lines_to_pair(lines):
    whole = jnp.concatenate(lines, axis=1)
    half = whole.shape[1] // 2
    return jnp.concatenate([whole[:, :half], whole[:, half:]], axis=0)


def upright(pair):
    count = 2 * pair.shape[1] // LANES
    block = jnp.concatenate([tile_of(pair, t) for t in range(count)] + [tile_of(pair, 0)] * (-count % 8), axis=0).T
    return jnp.concatenate([jnp.broadcast_to(block[:, t : t + 1], (LANES, LANES)) for t in range(count)], axis=0)


def two_terms(line):
    high = line.astype(BF16).astype(F32)
    row = lax.broadcasted_iota(jnp.int32, (16, line.shape[1]), 0)
    return jnp.where(row == 0, high, jnp.where(row == 1, line - high, 0.0)).astype(BF16)


def read_mode(ref, m, modes, owned, halves):
    per_owner = halves * modes * owned
    count = ref.shape[0] // per_owner
    parts = [
        jnp.concatenate(
            [ref[pl.ds((h * modes + m) * owned + i, count, stride=per_owner), :] for h in range(halves)], axis=1
        )
        for i in range(owned)
    ]
    return jnp.concatenate(parts, axis=0)


def score_body(modes, owned, rows_ref, protos_ref, kernel_ref, units_ref, unit_protos_ref, soft_ref, mass_ref, rows32):
    samples = units_ref.shape[0] // modes
    width = protos_ref.shape[0]
    halves = protos_ref.shape[1] // LANES
    raw = protos_ref[...].astype(F32)
    scale = lax.rsqrt(jnp.sum(raw * raw, axis=-1, keepdims=True) + 1e-6)
    unit_protos_ref[...] = (raw * scale).astype(BF16)
    rows32[...] = rows_ref[...].astype(F32)
    lines = []
    for m in range(modes):
        rows = slice(m * samples, (m + 1) * samples)
        raw = read_mode(rows32, m, modes, owned, halves)
        units = (raw * lax.rsqrt(jnp.sum(raw * raw, axis=-1, keepdims=True) + 1e-6)).astype(BF16)
        units_ref[rows, :] = units
        scores = lax.dot_general(units, unit_protos_ref[...], NT, preferred_element_type=F32)
        soft = jnp.exp(scores * 10.0)
        kernel = soft * soft
        kernel_ref[rows, :] = kernel.astype(BF16)
        line_to_tiles(mass_ref, m * (width // LANES), jnp.sum(kernel, axis=0, keepdims=True))
        folded = soft[:, :LANES]
        for j in range(1, width // LANES):
            folded = folded + soft[:, j * LANES : (j + 1) * LANES]
        high = folded.astype(BF16)
        low = (folded - high.astype(F32)).astype(BF16)
        ones = jnp.ones((16, LANES), BF16)
        line = lax.dot_general(ones, high, NT, preferred_element_type=F32)
        line = line + lax.dot_general(ones, low, NT, preferred_element_type=F32)
        lines.append(line[0:1])
    soft_ref[...] = lines_to_pair(lines)


def row_body(modes, mass_ref, kernel_ref, row_ref, inverse_ref):
    samples = kernel_ref.shape[0] // modes
    tiles = kernel_ref.shape[1] // LANES
    inverse = 1.0 / mass_ref[...]
    inverse_ref[...] = inverse
    lines = []
    for m in range(modes):
        terms = two_terms(tiles_to_line(inverse, m * tiles, tiles))
        kernel = kernel_ref[m * samples : (m + 1) * samples, :]
        line = lax.dot_general(terms, kernel, NT, preferred_element_type=F32)
        lines.append(line[0:1] + line[1:2])
    row_ref[...] = lines_to_pair(lines)


def column_body(modes, row_ref, kernel_ref, mass_ref):
    samples = kernel_ref.shape[0] // modes
    width = kernel_ref.shape[1]
    weight = 1.0 / row_ref[...]
    for m in range(modes):
        terms = two_terms(mode_of(weight, m, samples // LANES))
        kernel = kernel_ref[m * samples : (m + 1) * samples, :]
        line = jnp.dot(terms, kernel, preferred_element_type=F32)
        line_to_tiles(mass_ref, m * (width // LANES), line[0:1] + line[1:2])


def unit_body(modes, owned, place_ref, totals_ref, inverse_ref, units_ref, unit_protos_ref, tied_ref, *refs):
    pieces, (weights, sums) = refs[:-2], refs[-2:]
    samples = units_ref.shape[0] // modes
    width = unit_protos_ref.shape[0]
    tiles = width // LANES
    chunk = samples // owned // len(pieces)
    weights[0] = upright(COEFFICIENT / totals_ref[0:2])
    weights[1] = upright(2.0 * COEFFICIENT / totals_ref[2:4])
    step = 512
    for k in range(0, width, step):
        protos = unit_protos_ref[k : k + step, :]
        scores = lax.dot_general(units_ref[...], protos, NT, preferred_element_type=F32)
        codes, predicted = [], []
        for m in range(modes):
            rows = slice(m * samples, (m + 1) * samples)
            soft = jnp.exp(10.0 * scores[rows])
            inverse = tiles_to_line(inverse_ref[...], m * tiles + k // LANES, step // LANES)
            codes.append(soft * soft * inverse * jnp.concatenate([weights[0, rows, :]] * (step // LANES), axis=1))
            predicted.append(soft * jnp.concatenate([weights[1, rows, :]] * (step // LANES), axis=1))
        for m in range(modes):
            rows = slice(m * samples, (m + 1) * samples)
            logit = predicted[m] - functools.reduce(jnp.add, [codes[n] for n in range(modes) if n != m])
            part = jnp.dot(logit.astype(BF16), protos, preferred_element_type=F32)
            sums[rows, :] = part if k == 0 else sums[rows, :] + part
    for step, piece in enumerate(pieces):
        place = lax.bitwise_xor(place_ref[0], jnp.int32(step)) * chunk
        for j in range(modes * owned):
            first = pl.multiple_of(place + j * (samples // owned), chunk)
            piece[j * chunk : (j + 1) * chunk, :] = sums[pl.ds(first, chunk), :].astype(BF16)


def proto_body(modes, totals_ref, inverse_ref, units_ref, unit_protos_ref, proto_ref):
    samples = units_ref.shape[0] // modes
    width = unit_protos_ref.shape[0]
    tiles = width // LANES
    inverse = inverse_ref[...].T
    weight = COEFFICIENT / totals_ref[0:2]
    spread = 2.0 * COEFFICIENT / totals_ref[2:4]
    weight = [mode_of(weight, m, samples // LANES) for m in range(modes)]
    spread = [mode_of(spread, m, samples // LANES) for m in range(modes)]
    step = 256
    for k in range(0, width, step):
        scores = lax.dot_general(unit_protos_ref[k : k + step, :], units_ref[...], NT, preferred_element_type=F32)
        codes, predicted = [], []
        for m in range(modes):
            first = m * tiles + k // LANES
            upright_inverse = jnp.concatenate([inverse[:, first + j : first + j + 1] for j in range(step // LANES)], axis=0)
            soft = jnp.exp(10.0 * scores[:, m * samples : (m + 1) * samples])
            codes.append(soft * soft * upright_inverse * weight[m])
            predicted.append(soft * spread[m])
        logit = [
            (predicted[m] - functools.reduce(jnp.add, [codes[n] for n in range(modes) if n != m])).astype(BF16)
            for m in range(modes)
        ]
        proto_ref[k : k + step, :] = jnp.dot(
            jnp.concatenate(logit, axis=1), units_ref[...], preferred_element_type=F32
        ).astype(BF16)


def middle_body(place_ref, parts_ref, protos_ref, *refs):
    pieces, (grad_ref, rows_ref, unit) = refs[:-3], refs[-3:]
    total = jnp.sum(parts_ref[...].astype(F32), axis=0)
    share = total.shape[0]
    raw = protos_ref[pl.ds(pl.multiple_of(place_ref[0] * share, share), share), :].astype(F32)
    scale = lax.rsqrt(jnp.sum(raw * raw, axis=-1, keepdims=True) + 1e-6)
    inner = jnp.sum(total * raw, axis=-1, keepdims=True)
    grad_ref[...] = (scale * total - scale * scale * scale * inner * raw).astype(BF16)
    total = functools.reduce(jnp.add, [piece[...].astype(F32) for piece in pieces])
    for h in range(unit.shape[0]):
        unit[h] = total[:, h * LANES : (h + 1) * LANES]
    cuts = rows_ref.shape[0]
    for j in range(cuts):
        rows_ref[j] = jnp.concatenate(
            [unit[h, pl.ds(j, unit.shape[1] // cuts, stride=cuts), :] for h in range(unit.shape[0])], axis=0
        ).astype(BF16)


def last_body(parts_ref, raw_ref, grad_ref):
    total = jnp.sum(parts_ref[...].astype(F32), axis=0)
    raw = raw_ref[...].astype(F32)
    count = raw.shape[0]
    total = jnp.concatenate([total[h : h + count] for h in range(0, total.shape[0], count)], axis=1)
    scale = lax.rsqrt(jnp.sum(raw * raw, axis=-1, keepdims=True) + 1e-6)
    inner = jnp.sum(total * raw, axis=-1, keepdims=True)
    grad = scale * total - scale * scale * scale * inner * raw
    modes, owned = grad_ref.shape[:2]
    for m in range(modes):
        grad_ref[m] = grad[m * owned : (m + 1) * owned]


def exchange(x, axes):
    return lax.all_to_all(x, axes, 0, 0, tiled=True)


def copies(x, axes, count):
    return exchange(jnp.broadcast_to(x[None], (count,) + x.shape), axes)


def gather(x, axes, count):
    return copies(x, axes, count).reshape((count * x.shape[0],) + x.shape[1:])


def sum_over(x, axes, count):
    return jnp.sum(copies(x.astype(BF16), axes, count).astype(F32), axis=0)


def swap(x, axis, count, step):
    return lax.ppermute(x, axis, [(i, i ^ step) for i in range(count)]) if step else x


def per_device(sizes, embeddings, prototypes):
    modes, width = embeddings.shape[1:]
    own_samples = embeddings.shape[0]
    owned = own_samples * modes
    local_protos = prototypes.shape[0]
    ny, nc, nx, nz = (sizes[a] for a in ("y", "core", "x", "z"))
    dp = ("y", "core")
    groups = ny * nc
    lines = owned * nx * nz
    x_lines = lines // nx
    mass_shape = shape((modes * local_protos // LANES, LANES), F32)
    row_shape = shape((2, lines // 2), F32)
    units_shape = shape((lines, width), BF16)
    dp_place = lax.axis_index(dp).reshape(1)
    x_place = lax.axis_index("x").reshape(1)

    row_call = call(functools.partial(row_body, modes), "row_sum", [row_shape, mass_shape], [WHOLE] * 2)
    column_call = call(functools.partial(column_body, modes), "column_sum", mass_shape, [WHOLE] * 2)

    raw_rows = embeddings.transpose(1, 0, 2).reshape(owned, width)
    raw_tiles = jnp.concatenate([raw_rows[:, h : h + LANES] for h in range(0, width, LANES)], axis=0)
    gathered = gather(gather(raw_tiles, "z", nz), "x", nx)
    kernel, units, unit_protos, soft, mass = call(
        functools.partial(score_body, modes, own_samples),
        "scores",
        [shape((lines, local_protos), BF16), units_shape, shape((local_protos, width), BF16), row_shape, mass_shape],
        [WHOLE] * 2,
        [pltpu.VMEM(gathered.shape, F32)],
    )(gathered, prototypes)

    for _ in range(2):
        row, _ = row_call(sum_over(mass, dp, groups), kernel)
        mass = column_call(sum_over(row, ("x", "z"), nx * nz), kernel)
    row, inverse = row_call(sum_over(mass, dp, groups), kernel)
    totals = sum_over(jnp.concatenate([row, soft], axis=0), ("x", "z"), nx * nz)

    proto_part = call(
        functools.partial(proto_body, modes), "proto_part", shape((local_protos, width), BF16), [WHOLE] * 4
    )(totals, inverse, units, unit_protos)
    pieces = call(
        functools.partial(unit_body, modes, own_samples),
        "unit_grad",
        [shape((x_lines, width), BF16)] * nx,
        [SCALARS] + [WHOLE] * 4 + [ANYWHERE],
        [pltpu.VMEM((2, lines, LANES), F32), pltpu.VMEM((lines, width), F32)],
    )(x_place, totals, inverse, units, unit_protos, proto_part)
    proto_part = exchange(proto_part, dp).reshape(groups, local_protos // groups, width)
    pieces = [swap(piece, "x", nx, step) for step, piece in enumerate(pieces)]
    proto_grad, rows = call(
        middle_body,
        "middle",
        [shape((local_protos // groups, width), BF16), shape((nz, owned * width // LANES, LANES), BF16)],
        [SCALARS] + [WHOLE] * (2 + nx),
        [pltpu.VMEM((width // LANES, x_lines, LANES), F32)],
    )(dp_place, proto_part, prototypes, *pieces)
    rows = exchange(rows, "z")
    proto_grad = lax.all_gather(proto_grad, dp, axis=0, tiled=True).astype(F32)
    embed_grad = call(last_body, "last", shape((modes, own_samples, width), F32), [WHOLE] * 2)(rows, raw_rows)
    return (embed_grad.transpose(1, 0, 2), proto_grad)


def solution(mesh):
    sizes = dict(y=mesh.shape["dp"] // 2, core=2, x=4, z=mesh.shape["proto"] // 4)
    fine = Mesh(mesh.devices.reshape(tuple(sizes.values())), tuple(sizes))
    specs = (P(("y", "core", "x", "z"), None, None), P(("x", "z"), None))
    return jax.shard_map(
        functools.partial(per_device, sizes), mesh=fine, in_specs=specs, out_specs=specs, check_vma=False
    )
```

```python
import functools

import jax
import jax.numpy as jnp
from jax import lax
from jax.experimental import pallas as pl
from jax.experimental.pallas import tpu as pltpu
from jax.sharding import Mesh, PartitionSpec as P

F32 = jnp.float32
BF16 = jnp.bfloat16
LANES = 128
COEFFICIENT = 64.0 * 10.0 / 6.0
NT = (((1,), (1,)), ((), ()))
SCALARS = pl.BlockSpec(memory_space=pltpu.SMEM)
WHOLE = pl.BlockSpec(memory_space=pltpu.VMEM)
ANYWHERE = pl.BlockSpec(memory_space=pl.ANY)


def call(body, name, out_shapes, in_specs, scratch=(), out_specs=None, aliases=None):
    many = isinstance(out_shapes, (list, tuple))
    return pl.pallas_call(
        body,
        name=name,
        in_specs=in_specs,
        out_shape=out_shapes,
        out_specs=out_specs or ([WHOLE] * len(out_shapes) if many else WHOLE),
        scratch_shapes=list(scratch),
        input_output_aliases=aliases or {},
        compiler_params=pltpu.CompilerParams(vmem_limit_bytes=28 * 1024 * 1024),
    )


def shape(dims, dtype):
    return jax.ShapeDtypeStruct(dims, dtype)


def tiles_to_line(block, first, count):
    return jnp.concatenate([block[first + j : first + j + 1] for j in range(count)], axis=1)


def line_to_tiles(ref, first, line):
    for j in range(line.shape[1] // LANES):
        ref[first + j : first + j + 1, :] = line[:, j * LANES : (j + 1) * LANES]


def tile_of(pair, tile):
    half = pair.shape[1] // LANES
    return pair[tile // half : tile // half + 1, (tile % half) * LANES : (tile % half + 1) * LANES]


def mode_of(pair, m, tiles):
    return jnp.concatenate([tile_of(pair, m * tiles + j) for j in range(tiles)], axis=1)


def lines_to_pair(lines):
    whole = jnp.concatenate(lines, axis=1)
    half = whole.shape[1] // 2
    return jnp.concatenate([whole[:, :half], whole[:, half:]], axis=0)


def upright(pair):
    count = 2 * pair.shape[1] // LANES
    block = jnp.concatenate([tile_of(pair, t) for t in range(count)] + [tile_of(pair, 0)] * (-count % 8), axis=0).T
    return jnp.concatenate([jnp.broadcast_to(block[:, t : t + 1], (LANES, LANES)) for t in range(count)], axis=0)


def two_terms(line):
    high = line.astype(BF16).astype(F32)
    row = lax.broadcasted_iota(jnp.int32, (16, line.shape[1]), 0)
    return jnp.where(row == 0, high, jnp.where(row == 1, line - high, 0.0)).astype(BF16)


def read_mode(ref, m, modes, owned, halves):
    per_owner = halves * modes * owned
    count = ref.shape[0] // per_owner
    parts = [
        jnp.concatenate(
            [ref[pl.ds((h * modes + m) * owned + i, count, stride=per_owner), :] for h in range(halves)], axis=1
        )
        for i in range(owned)
    ]
    return jnp.concatenate(parts, axis=0)


def score_body(modes, owned, rows_ref, protos_ref, kernel_ref, units_ref, unit_protos_ref, soft_ref, mass_ref, rows32):
    samples = units_ref.shape[0] // modes
    width = protos_ref.shape[0]
    halves = protos_ref.shape[1] // LANES
    raw = protos_ref[...].astype(F32)
    scale = lax.rsqrt(jnp.sum(raw * raw, axis=-1, keepdims=True) + 1e-6)
    unit_protos_ref[...] = (raw * scale).astype(BF16)
    rows32[...] = rows_ref[...].astype(F32)
    lines = []
    for m in range(modes):
        rows = slice(m * samples, (m + 1) * samples)
        raw = read_mode(rows32, m, modes, owned, halves)
        units = (raw * lax.rsqrt(jnp.sum(raw * raw, axis=-1, keepdims=True) + 1e-6)).astype(BF16)
        units_ref[rows, :] = units
        scores = lax.dot_general(units, unit_protos_ref[...], NT, preferred_element_type=F32)
        soft = jnp.exp(scores * 10.0)
        kernel = soft * soft
        kernel_ref[rows, :] = kernel.astype(BF16)
        line_to_tiles(mass_ref, m * (width // LANES), jnp.sum(kernel, axis=0, keepdims=True))
        folded = soft[:, :LANES]
        for j in range(1, width // LANES):
            folded = folded + soft[:, j * LANES : (j + 1) * LANES]
        high = folded.astype(BF16)
        low = (folded - high.astype(F32)).astype(BF16)
        ones = jnp.ones((16, LANES), BF16)
        line = lax.dot_general(ones, high, NT, preferred_element_type=F32)
        line = line + lax.dot_general(ones, low, NT, preferred_element_type=F32)
        lines.append(line[0:1])
    soft_ref[...] = lines_to_pair(lines)


def row_body(modes, mass_ref, kernel_ref, *refs):
    samples = kernel_ref.shape[0] // modes
    tiles = kernel_ref.shape[1] // LANES
    inverse = 1.0 / mass_ref[...]
    lines = []
    for m in range(modes):
        terms = two_terms(tiles_to_line(inverse, m * tiles, tiles))
        kernel = kernel_ref[m * samples : (m + 1) * samples, :]
        line = lax.dot_general(terms, kernel, NT, preferred_element_type=F32)
        lines.append(line[0:1] + line[1:2])
    pair = lines_to_pair(lines)
    if len(refs) == 1:
        refs[0][...] = pair
    else:
        soft_ref, row_ref, inverse_ref = refs
        row_ref[...] = jnp.concatenate([pair, soft_ref[...]], axis=0)
        inverse_ref[...] = inverse


def column_body(modes, row_ref, kernel_ref, mass_ref):
    samples = kernel_ref.shape[0] // modes
    width = kernel_ref.shape[1]
    weight = 1.0 / row_ref[...]
    for m in range(modes):
        terms = two_terms(mode_of(weight, m, samples // LANES))
        kernel = kernel_ref[m * samples : (m + 1) * samples, :]
        line = jnp.dot(terms, kernel, preferred_element_type=F32)
        line_to_tiles(mass_ref, m * (width // LANES), line[0:1] + line[1:2])


def unit_body(modes, owned, place_ref, totals_ref, inverse_ref, units_ref, unit_protos_ref, tied_ref, *refs):
    pieces, (weights, sums) = refs[:-2], refs[-2:]
    samples = units_ref.shape[0] // modes
    width = unit_protos_ref.shape[0]
    tiles = width // LANES
    chunk = samples // owned // len(pieces)
    weights[0] = upright(COEFFICIENT / totals_ref[0:2])
    weights[1] = upright(2.0 * COEFFICIENT / totals_ref[2:4])
    step = 512
    for k in range(0, width, step):
        protos = unit_protos_ref[k : k + step, :]
        scores = lax.dot_general(units_ref[...], protos, NT, preferred_element_type=F32)
        codes, predicted = [], []
        for m in range(modes):
            rows = slice(m * samples, (m + 1) * samples)
            soft = jnp.exp(10.0 * scores[rows])
            inverse = tiles_to_line(inverse_ref[...], m * tiles + k // LANES, step // LANES)
            codes.append(soft * soft * inverse * jnp.concatenate([weights[0, rows, :]] * (step // LANES), axis=1))
            predicted.append(soft * jnp.concatenate([weights[1, rows, :]] * (step // LANES), axis=1))
        for m in range(modes):
            rows = slice(m * samples, (m + 1) * samples)
            logit = predicted[m] - functools.reduce(jnp.add, [codes[n] for n in range(modes) if n != m])
            part = jnp.dot(logit.astype(BF16), protos, preferred_element_type=F32)
            sums[rows, :] = part if k == 0 else sums[rows, :] + part
    for step, piece in enumerate(pieces):
        place = lax.bitwise_xor(place_ref[0], jnp.int32(step)) * chunk
        for j in range(modes * owned):
            first = pl.multiple_of(place + j * (samples // owned), chunk)
            piece[j * chunk : (j + 1) * chunk, :] = sums[pl.ds(first, chunk), :].astype(BF16)


def proto_body(modes, totals_ref, inverse_ref, units_ref, unit_protos_ref, proto_ref):
    samples = units_ref.shape[0] // modes
    width = unit_protos_ref.shape[0]
    tiles = width // LANES
    inverse = inverse_ref[...].T
    weight = COEFFICIENT / totals_ref[0:2]
    spread = 2.0 * COEFFICIENT / totals_ref[2:4]
    weight = [mode_of(weight, m, samples // LANES) for m in range(modes)]
    spread = [mode_of(spread, m, samples // LANES) for m in range(modes)]
    step = 256
    for k in range(0, width, step):
        scores = lax.dot_general(unit_protos_ref[k : k + step, :], units_ref[...], NT, preferred_element_type=F32)
        codes, predicted = [], []
        for m in range(modes):
            first = m * tiles + k // LANES
            upright_inverse = jnp.concatenate([inverse[:, first + j : first + j + 1] for j in range(step // LANES)], axis=0)
            soft = jnp.exp(10.0 * scores[:, m * samples : (m + 1) * samples])
            codes.append(soft * soft * upright_inverse * weight[m])
            predicted.append(soft * spread[m])
        logit = [
            (predicted[m] - functools.reduce(jnp.add, [codes[n] for n in range(modes) if n != m])).astype(BF16)
            for m in range(modes)
        ]
        proto_ref[k : k + step, :] = jnp.dot(
            jnp.concatenate(logit, axis=1), units_ref[...], preferred_element_type=F32
        ).astype(BF16)


def middle_body(place_ref, parts_ref, protos_ref, *refs):
    pieces, (grad_ref, rows_ref, unit) = refs[:-3], refs[-3:]
    total = jnp.sum(parts_ref[...].astype(F32), axis=0)
    share = total.shape[0]
    raw = protos_ref[pl.ds(pl.multiple_of(place_ref[0] * share, share), share), :].astype(F32)
    scale = lax.rsqrt(jnp.sum(raw * raw, axis=-1, keepdims=True) + 1e-6)
    inner = jnp.sum(total * raw, axis=-1, keepdims=True)
    grad_ref[...] = (scale * total - scale * scale * scale * inner * raw).astype(BF16)
    total = functools.reduce(jnp.add, [piece[...].astype(F32) for piece in pieces])
    for h in range(unit.shape[0]):
        unit[h] = total[:, h * LANES : (h + 1) * LANES]
    cuts = rows_ref.shape[0]
    for j in range(cuts):
        rows_ref[j] = jnp.concatenate(
            [unit[h, pl.ds(j, unit.shape[1] // cuts, stride=cuts), :] for h in range(unit.shape[0])], axis=0
        ).astype(BF16)


def last_body(parts_ref, raw_ref, protos_ref, grad_ref, proto_grad_ref):
    proto_grad_ref[...] = protos_ref[...].astype(F32)
    total = jnp.sum(parts_ref[...].astype(F32), axis=0)
    raw = raw_ref[...].astype(F32)
    count = raw.shape[0]
    total = jnp.concatenate([total[h : h + count] for h in range(0, total.shape[0], count)], axis=1)
    scale = lax.rsqrt(jnp.sum(raw * raw, axis=-1, keepdims=True) + 1e-6)
    inner = jnp.sum(total * raw, axis=-1, keepdims=True)
    grad = scale * total - scale * scale * scale * inner * raw
    modes, owned = grad_ref.shape[:2]
    for m in range(modes):
        grad_ref[m] = grad[m * owned : (m + 1) * owned]


def exchange(x, axes):
    return lax.all_to_all(x, axes, 0, 0, tiled=True)


def copies(x, axes, count):
    return exchange(jnp.broadcast_to(x[None], (count,) + x.shape), axes)


def gather(x, axes, count):
    return copies(x, axes, count).reshape((count * x.shape[0],) + x.shape[1:])


def sum_over(x, axes, count):
    return jnp.sum(copies(x.astype(BF16), axes, count).astype(F32), axis=0)


def swap(x, axis, count, step):
    return lax.ppermute(x, axis, [(i, i ^ step) for i in range(count)]) if step else x


def per_device(sizes, embeddings, prototypes):
    modes, width = embeddings.shape[1:]
    own_samples = embeddings.shape[0]
    owned = own_samples * modes
    local_protos = prototypes.shape[0]
    ny, nc, nx, nz = (sizes[a] for a in ("y", "core", "x", "z"))
    dp = ("y", "core")
    groups = ny * nc
    lines = owned * nx * nz
    x_lines = lines // nx
    mass_shape = shape((modes * local_protos // LANES, LANES), F32)
    row_shape = shape((2, lines // 2), F32)
    units_shape = shape((lines, width), BF16)
    dp_place = lax.axis_index(dp).reshape(1)
    x_place = lax.axis_index("x").reshape(1)

    row_call = call(functools.partial(row_body, modes), "row_sum", row_shape, [WHOLE] * 2)
    last_row_call = call(
        functools.partial(row_body, modes), "row_sum", [shape((4, lines // 2), F32), mass_shape], [WHOLE] * 3
    )
    column_call = call(functools.partial(column_body, modes), "column_sum", mass_shape, [WHOLE] * 2)

    raw_rows = embeddings.transpose(1, 0, 2).reshape(owned, width)
    raw_tiles = jnp.concatenate([raw_rows[:, h : h + LANES] for h in range(0, width, LANES)], axis=0)
    gathered = gather(gather(raw_tiles, "z", nz), "x", nx)
    kernel, units, unit_protos, soft, mass = call(
        functools.partial(score_body, modes, own_samples),
        "scores",
        [shape((lines, local_protos), BF16), units_shape, shape((local_protos, width), BF16), row_shape, mass_shape],
        [WHOLE] * 2,
        [pltpu.VMEM(gathered.shape, F32)],
    )(gathered, prototypes)

    for _ in range(2):
        row = row_call(sum_over(mass, dp, groups), kernel)
        mass = column_call(sum_over(row, ("x", "z"), nx * nz), kernel)
    row, inverse = last_row_call(sum_over(mass, dp, groups), kernel, soft)
    totals = sum_over(row, ("x", "z"), nx * nz)

    proto_part = call(
        functools.partial(proto_body, modes), "proto_part", shape((local_protos, width), BF16), [WHOLE] * 4
    )(totals, inverse, units, unit_protos)
    pieces = call(
        functools.partial(unit_body, modes, own_samples),
        "unit_grad",
        [shape((x_lines, width), BF16)] * nx,
        [SCALARS] + [WHOLE] * 4 + [ANYWHERE],
        [pltpu.VMEM((2, lines, LANES), F32), pltpu.VMEM((lines, width), F32)],
    )(x_place, totals, inverse, units, unit_protos, proto_part)
    proto_part = exchange(proto_part, dp).reshape(groups, local_protos // groups, width)
    pieces = [swap(piece, "x", nx, step) for step, piece in enumerate(pieces)]
    proto_grad, rows = call(
        middle_body,
        "middle",
        [shape((local_protos // groups, width), BF16), shape((nz, owned * width // LANES, LANES), BF16)],
        [SCALARS] + [WHOLE] * (2 + nx),
        [pltpu.VMEM((width // LANES, x_lines, LANES), F32)],
    )(dp_place, proto_part, prototypes, *pieces)
    rows = exchange(rows, "z")
    proto_grad = lax.all_gather(proto_grad, dp, axis=0, tiled=True)
    embed_grad, proto_grad = call(
        last_body,
        "last",
        [shape((modes, own_samples, width), F32), shape((local_protos, width), F32)],
        [WHOLE] * 3,
    )(rows, raw_rows, proto_grad)
    return (embed_grad.transpose(1, 0, 2), proto_grad)


def solution(mesh):
    sizes = dict(y=mesh.shape["dp"] // 2, core=2, x=4, z=mesh.shape["proto"] // 4)
    fine = Mesh(mesh.devices.reshape(tuple(sizes.values())), tuple(sizes))
    specs = (P(("y", "core", "x", "z"), None, None), P(("x", "z"), None))
    return jax.shard_map(
        functools.partial(per_device, sizes), mesh=fine, in_specs=specs, out_specs=specs, check_vma=False
    )
```

```python
import functools

import jax
import jax.numpy as jnp
from jax import lax
from jax.experimental import pallas as pl
from jax.experimental.pallas import tpu as pltpu
from jax.sharding import Mesh, PartitionSpec as P

F32 = jnp.float32
BF16 = jnp.bfloat16
LANES = 128
COEFFICIENT = 64.0 * 10.0 / 6.0
NT = (((1,), (1,)), ((), ()))
SCALARS = pl.BlockSpec(memory_space=pltpu.SMEM)
WHOLE = pl.BlockSpec(memory_space=pltpu.VMEM)
ANYWHERE = pl.BlockSpec(memory_space=pl.ANY)


def call(body, name, out_shapes, in_specs, scratch=(), out_specs=None, aliases=None):
    many = isinstance(out_shapes, (list, tuple))
    return pl.pallas_call(
        body,
        name=name,
        in_specs=in_specs,
        out_shape=out_shapes,
        out_specs=out_specs or ([WHOLE] * len(out_shapes) if many else WHOLE),
        scratch_shapes=list(scratch),
        input_output_aliases=aliases or {},
        compiler_params=pltpu.CompilerParams(vmem_limit_bytes=28 * 1024 * 1024),
    )


def shape(dims, dtype):
    return jax.ShapeDtypeStruct(dims, dtype)


def tiles_to_line(block, first, count):
    return jnp.concatenate([block[first + j : first + j + 1] for j in range(count)], axis=1)


def line_to_tiles(ref, first, line):
    for j in range(line.shape[1] // LANES):
        ref[first + j : first + j + 1, :] = line[:, j * LANES : (j + 1) * LANES]


def tile_of(pair, tile):
    half = pair.shape[1] // LANES
    return pair[tile // half : tile // half + 1, (tile % half) * LANES : (tile % half + 1) * LANES]


def mode_of(pair, m, tiles):
    return jnp.concatenate([tile_of(pair, m * tiles + j) for j in range(tiles)], axis=1)


def lines_to_pair(lines):
    whole = jnp.concatenate(lines, axis=1)
    half = whole.shape[1] // 2
    return jnp.concatenate([whole[:, :half], whole[:, half:]], axis=0)


def upright(pair):
    count = 2 * pair.shape[1] // LANES
    block = jnp.concatenate([tile_of(pair, t) for t in range(count)] + [tile_of(pair, 0)] * (-count % 8), axis=0).T
    return jnp.concatenate([jnp.broadcast_to(block[:, t : t + 1], (LANES, LANES)) for t in range(count)], axis=0)


def two_terms(line):
    high = line.astype(BF16).astype(F32)
    row = lax.broadcasted_iota(jnp.int32, (16, line.shape[1]), 0)
    return jnp.where(row == 0, high, jnp.where(row == 1, line - high, 0.0)).astype(BF16)


def read_mode(ref, m, modes, owned, halves):
    per_owner = halves * modes * owned
    count = ref.shape[0] // per_owner
    parts = [
        jnp.concatenate(
            [ref[pl.ds((h * modes + m) * owned + i, count, stride=per_owner), :] for h in range(halves)], axis=1
        )
        for i in range(owned)
    ]
    return jnp.concatenate(parts, axis=0)


def score_body(modes, owned, rows_ref, protos_ref, kernel_ref, soft_kernel_ref, units_ref, unit_protos_ref, soft_ref, mass_ref, rows32):
    samples = units_ref.shape[0] // modes
    width = protos_ref.shape[0]
    halves = protos_ref.shape[1] // LANES
    raw = protos_ref[...].astype(F32)
    scale = lax.rsqrt(jnp.sum(raw * raw, axis=-1, keepdims=True) + 1e-6)
    unit_protos_ref[...] = (raw * scale).astype(BF16)
    rows32[...] = rows_ref[...].astype(F32)
    lines = []
    for m in range(modes):
        rows = slice(m * samples, (m + 1) * samples)
        raw = read_mode(rows32, m, modes, owned, halves)
        units = (raw * lax.rsqrt(jnp.sum(raw * raw, axis=-1, keepdims=True) + 1e-6)).astype(BF16)
        units_ref[rows, :] = units
        scores = lax.dot_general(units, unit_protos_ref[...], NT, preferred_element_type=F32)
        soft = jnp.exp(scores * 10.0)
        kernel = soft * soft
        kernel_ref[rows, :] = kernel.astype(BF16)
        soft_kernel_ref[rows, :] = soft.astype(BF16)
        line_to_tiles(mass_ref, m * (width // LANES), jnp.sum(kernel, axis=0, keepdims=True))
        folded = soft[:, :LANES]
        for j in range(1, width // LANES):
            folded = folded + soft[:, j * LANES : (j + 1) * LANES]
        high = folded.astype(BF16)
        low = (folded - high.astype(F32)).astype(BF16)
        ones = jnp.ones((16, LANES), BF16)
        line = lax.dot_general(ones, high, NT, preferred_element_type=F32)
        line = line + lax.dot_general(ones, low, NT, preferred_element_type=F32)
        lines.append(line[0:1])
    soft_ref[...] = lines_to_pair(lines)


def row_body(modes, mass_ref, kernel_ref, *refs):
    samples = kernel_ref.shape[0] // modes
    tiles = kernel_ref.shape[1] // LANES
    inverse = 1.0 / mass_ref[...]
    lines = []
    for m in range(modes):
        terms = two_terms(tiles_to_line(inverse, m * tiles, tiles))
        kernel = kernel_ref[m * samples : (m + 1) * samples, :]
        line = lax.dot_general(terms, kernel, NT, preferred_element_type=F32)
        lines.append(line[0:1] + line[1:2])
    pair = lines_to_pair(lines)
    if len(refs) == 1:
        refs[0][...] = pair
    else:
        soft_ref, row_ref, inverse_ref = refs
        row_ref[...] = jnp.concatenate([pair, soft_ref[...]], axis=0)
        inverse_ref[...] = inverse


def column_body(modes, row_ref, kernel_ref, mass_ref):
    samples = kernel_ref.shape[0] // modes
    width = kernel_ref.shape[1]
    weight = 1.0 / row_ref[...]
    for m in range(modes):
        terms = two_terms(mode_of(weight, m, samples // LANES))
        kernel = kernel_ref[m * samples : (m + 1) * samples, :]
        line = jnp.dot(terms, kernel, preferred_element_type=F32)
        line_to_tiles(mass_ref, m * (width // LANES), line[0:1] + line[1:2])


def upright_factors(totals_ref, width):
    return [
        jnp.concatenate([upright(factor)] * (width // LANES), axis=1)
        for factor in (COEFFICIENT / totals_ref[0:2], 2.0 * COEFFICIENT / totals_ref[2:4])
    ]


def all_but(values, m):
    return functools.reduce(jnp.add, [values[n] for n in range(len(values)) if n != m])


def unit_body(modes, owned, place_ref, totals_ref, inverse_ref, soft_ref, kernel_ref, unit_protos_ref, tied_ref, *refs):
    pieces, sums = refs[:-1], refs[-1]
    samples = kernel_ref.shape[0] // modes
    tiles = kernel_ref.shape[1] // LANES
    chunk = samples // owned // len(pieces)
    weight, spread = upright_factors(totals_ref, unit_protos_ref.shape[1])
    codes, predicted = [], []
    for m in range(modes):
        rows = slice(m * samples, (m + 1) * samples)
        inverse = tiles_to_line(inverse_ref[...], m * tiles, tiles)
        assigned = (kernel_ref[rows, :].astype(F32) * inverse).astype(BF16)
        codes.append(weight[rows] * jnp.dot(assigned, unit_protos_ref[...], preferred_element_type=F32))
        predicted.append(spread[rows] * jnp.dot(soft_ref[rows, :], unit_protos_ref[...], preferred_element_type=F32))
    for m in range(modes):
        sums[m * samples : (m + 1) * samples, :] = predicted[m] - all_but(codes, m)
    for step, piece in enumerate(pieces):
        place = lax.bitwise_xor(place_ref[0], jnp.int32(step)) * chunk
        for j in range(modes * owned):
            first = pl.multiple_of(place + j * (samples // owned), chunk)
            piece[j * chunk : (j + 1) * chunk, :] = sums[pl.ds(first, chunk), :].astype(BF16)


def proto_body(modes, totals_ref, inverse_ref, units_ref, soft_ref, kernel_ref, proto_ref):
    samples = units_ref.shape[0] // modes
    width = kernel_ref.shape[1]
    tiles = width // LANES
    weight, spread = upright_factors(totals_ref, units_ref.shape[1])
    units = [units_ref[m * samples : (m + 1) * samples, :].astype(F32) for m in range(modes)]
    rows = [slice(m * samples, (m + 1) * samples) for m in range(modes)]
    for_codes = [(weight[rows[m]] * all_but(units, m)).T.astype(BF16) for m in range(modes)]
    for_predicted = [(spread[rows[m]] * units[m]).T.astype(BF16) for m in range(modes)]
    step = 256
    for k in range(0, width, step):
        total = jnp.zeros((units_ref.shape[1], step), F32)
        for m in range(modes):
            inverse = tiles_to_line(inverse_ref[...], m * tiles + k // LANES, step // LANES)
            total = total + jnp.dot(for_predicted[m], soft_ref[rows[m], k : k + step], preferred_element_type=F32)
            total = total - inverse * jnp.dot(for_codes[m], kernel_ref[rows[m], k : k + step], preferred_element_type=F32)
        proto_ref[k : k + step, :] = total.T.astype(BF16)


def middle_body(place_ref, parts_ref, protos_ref, *refs):
    pieces, (grad_ref, rows_ref, unit) = refs[:-3], refs[-3:]
    total = jnp.sum(parts_ref[...].astype(F32), axis=0)
    share = total.shape[0]
    raw = protos_ref[pl.ds(pl.multiple_of(place_ref[0] * share, share), share), :].astype(F32)
    scale = lax.rsqrt(jnp.sum(raw * raw, axis=-1, keepdims=True) + 1e-6)
    inner = jnp.sum(total * raw, axis=-1, keepdims=True)
    grad_ref[...] = (scale * total - scale * scale * scale * inner * raw).astype(BF16)
    total = functools.reduce(jnp.add, [piece[...].astype(F32) for piece in pieces])
    for h in range(unit.shape[0]):
        unit[h] = total[:, h * LANES : (h + 1) * LANES]
    cuts = rows_ref.shape[0]
    for j in range(cuts):
        rows_ref[j] = jnp.concatenate(
            [unit[h, pl.ds(j, unit.shape[1] // cuts, stride=cuts), :] for h in range(unit.shape[0])], axis=0
        ).astype(BF16)


def last_body(parts_ref, raw_ref, protos_ref, grad_ref, proto_grad_ref):
    proto_grad_ref[...] = protos_ref[...].astype(F32)
    total = jnp.sum(parts_ref[...].astype(F32), axis=0)
    raw = raw_ref[...].astype(F32)
    count = raw.shape[0]
    total = jnp.concatenate([total[h : h + count] for h in range(0, total.shape[0], count)], axis=1)
    scale = lax.rsqrt(jnp.sum(raw * raw, axis=-1, keepdims=True) + 1e-6)
    inner = jnp.sum(total * raw, axis=-1, keepdims=True)
    grad = scale * total - scale * scale * scale * inner * raw
    modes, owned = grad_ref.shape[:2]
    for m in range(modes):
        grad_ref[m] = grad[m * owned : (m + 1) * owned]


def exchange(x, axes):
    return lax.all_to_all(x, axes, 0, 0, tiled=True)


def copies(x, axes, count):
    return exchange(jnp.broadcast_to(x[None], (count,) + x.shape), axes)


def gather(x, axes, count):
    return copies(x, axes, count).reshape((count * x.shape[0],) + x.shape[1:])


def sum_over(x, axes, count):
    return jnp.sum(copies(x.astype(BF16), axes, count).astype(F32), axis=0)


def swap(x, axis, count, step):
    return lax.ppermute(x, axis, [(i, i ^ step) for i in range(count)]) if step else x


def per_device(sizes, embeddings, prototypes):
    modes, width = embeddings.shape[1:]
    own_samples = embeddings.shape[0]
    owned = own_samples * modes
    local_protos = prototypes.shape[0]
    ny, nc, nx, nz = (sizes[a] for a in ("y", "core", "x", "z"))
    dp = ("y", "core")
    groups = ny * nc
    lines = owned * nx * nz
    x_lines = lines // nx
    mass_shape = shape((modes * local_protos // LANES, LANES), F32)
    row_shape = shape((2, lines // 2), F32)
    units_shape = shape((lines, width), BF16)
    dp_place = lax.axis_index(dp).reshape(1)
    x_place = lax.axis_index("x").reshape(1)

    row_call = call(functools.partial(row_body, modes), "row_sum", row_shape, [WHOLE] * 2)
    last_row_call = call(
        functools.partial(row_body, modes), "row_sum", [shape((4, lines // 2), F32), mass_shape], [WHOLE] * 3
    )
    column_call = call(functools.partial(column_body, modes), "column_sum", mass_shape, [WHOLE] * 2)

    raw_rows = embeddings.transpose(1, 0, 2).reshape(owned, width)
    raw_tiles = jnp.concatenate([raw_rows[:, h : h + LANES] for h in range(0, width, LANES)], axis=0)
    gathered = gather(gather(raw_tiles, "z", nz), "x", nx)
    kernel, soft_kernel, units, unit_protos, soft, mass = call(
        functools.partial(score_body, modes, own_samples),
        "scores",
        [shape((lines, local_protos), BF16)] * 2 + [units_shape, shape((local_protos, width), BF16), row_shape, mass_shape],
        [WHOLE] * 2,
        [pltpu.VMEM(gathered.shape, F32)],
    )(gathered, prototypes)

    for _ in range(2):
        row = row_call(sum_over(mass, dp, groups), kernel)
        mass = column_call(sum_over(row, ("x", "z"), nx * nz), kernel)
    row, inverse = last_row_call(sum_over(mass, dp, groups), kernel, soft)
    totals = sum_over(row, ("x", "z"), nx * nz)

    proto_part = call(
        functools.partial(proto_body, modes), "proto_part", shape((local_protos, width), BF16), [WHOLE] * 5
    )(totals, inverse, units, soft_kernel, kernel)
    pieces = call(
        functools.partial(unit_body, modes, own_samples),
        "unit_grad",
        [shape((x_lines, width), BF16)] * nx,
        [SCALARS] + [WHOLE] * 5 + [ANYWHERE],
        [pltpu.VMEM((lines, width), F32)],
    )(x_place, totals, inverse, soft_kernel, kernel, unit_protos, proto_part)
    proto_part = exchange(proto_part, dp).reshape(groups, local_protos // groups, width)
    pieces = [pieces[0]] + [swap(pieces[step], "x", nx, step) for step in (2, 1, 3)]
    proto_grad, rows = call(
        middle_body,
        "middle",
        [shape((local_protos // groups, width), BF16), shape((nz, owned * width // LANES, LANES), BF16)],
        [SCALARS] + [WHOLE] * (2 + nx),
        [pltpu.VMEM((width // LANES, x_lines, LANES), F32)],
    )(dp_place, proto_part, prototypes, *pieces)
    rows = exchange(rows, "z")
    proto_grad = lax.all_gather(proto_grad, dp, axis=0, tiled=True)
    embed_grad, proto_grad = call(
        last_body,
        "last",
        [shape((modes, own_samples, width), F32), shape((local_protos, width), F32)],
        [WHOLE] * 3,
    )(rows, raw_rows, proto_grad)
    return (embed_grad.transpose(1, 0, 2), proto_grad)


def solution(mesh):
    sizes = dict(y=mesh.shape["dp"] // 2, core=2, x=4, z=mesh.shape["proto"] // 4)
    fine = Mesh(mesh.devices.reshape(tuple(sizes.values())), tuple(sizes))
    specs = (P(("y", "core", "x", "z"), None, None), P(("x", "z"), None))
    return jax.shard_map(
        functools.partial(per_device, sizes), mesh=fine, in_specs=specs, out_specs=specs, check_vma=False
    )
```

```python
import functools

import jax
import jax.numpy as jnp
from jax import lax
from jax.experimental import pallas as pl
from jax.experimental.pallas import tpu as pltpu
from jax.sharding import Mesh, PartitionSpec as P

F32 = jnp.float32
BF16 = jnp.bfloat16
LANES = 128
COEFFICIENT = 64.0 * 10.0 / 6.0
NT = (((1,), (1,)), ((), ()))
SCALARS = pl.BlockSpec(memory_space=pltpu.SMEM)
WHOLE = pl.BlockSpec(memory_space=pltpu.VMEM)
ANYWHERE = pl.BlockSpec(memory_space=pl.ANY)


def call(body, name, out_shapes, in_specs, scratch=(), out_specs=None, aliases=None):
    many = isinstance(out_shapes, (list, tuple))
    return pl.pallas_call(
        body,
        name=name,
        in_specs=in_specs,
        out_shape=out_shapes,
        out_specs=out_specs or ([WHOLE] * len(out_shapes) if many else WHOLE),
        scratch_shapes=list(scratch),
        input_output_aliases=aliases or {},
        compiler_params=pltpu.CompilerParams(vmem_limit_bytes=28 * 1024 * 1024),
    )


def shape(dims, dtype):
    return jax.ShapeDtypeStruct(dims, dtype)


def tiles_to_line(block, first, count):
    return jnp.concatenate([block[first + j : first + j + 1] for j in range(count)], axis=1)


def line_to_tiles(ref, first, line):
    for j in range(line.shape[1] // LANES):
        ref[first + j : first + j + 1, :] = line[:, j * LANES : (j + 1) * LANES]


def tile_of(pair, tile):
    half = pair.shape[1] // LANES
    return pair[tile // half : tile // half + 1, (tile % half) * LANES : (tile % half + 1) * LANES]


def mode_of(pair, m, tiles):
    return jnp.concatenate([tile_of(pair, m * tiles + j) for j in range(tiles)], axis=1)


def lines_to_pair(lines):
    whole = jnp.concatenate(lines, axis=1)
    half = whole.shape[1] // 2
    return jnp.concatenate([whole[:, :half], whole[:, half:]], axis=0)


def upright(pair):
    count = 2 * pair.shape[1] // LANES
    block = jnp.concatenate([tile_of(pair, t) for t in range(count)] + [tile_of(pair, 0)] * (-count % 8), axis=0).T
    return jnp.concatenate([jnp.broadcast_to(block[:, t : t + 1], (LANES, LANES)) for t in range(count)], axis=0)


def two_terms(line):
    high = line.astype(BF16).astype(F32)
    row = lax.broadcasted_iota(jnp.int32, (16, line.shape[1]), 0)
    return jnp.where(row == 0, high, jnp.where(row == 1, line - high, 0.0)).astype(BF16)


def read_mode(ref, m, modes, owned, halves):
    per_owner = halves * modes * owned
    count = ref.shape[0] // per_owner
    parts = [
        jnp.concatenate(
            [ref[pl.ds((h * modes + m) * owned + i, count, stride=per_owner), :] for h in range(halves)], axis=1
        )
        for i in range(owned)
    ]
    return jnp.concatenate(parts, axis=0)


def score_body(
    modes, owned, place_ref, rows_ref, protos_ref,
    kernel_ref, soft_kernel_ref, units_ref, unit_protos_ref, soft_ref, mass_ref, share_ref, rows32,
):
    samples = units_ref.shape[0] // modes
    width = protos_ref.shape[0]
    halves = protos_ref.shape[1] // LANES
    share = share_ref.shape[0]
    share_ref[...] = protos_ref[pl.ds(pl.multiple_of(place_ref[0] * share, share), share), :]
    raw = protos_ref[...].astype(F32)
    scale = lax.rsqrt(jnp.sum(raw * raw, axis=-1, keepdims=True) + 1e-6)
    unit_protos_ref[...] = (raw * scale).astype(BF16)
    rows32[...] = rows_ref[...].astype(F32)
    lines = []
    for m in range(modes):
        rows = slice(m * samples, (m + 1) * samples)
        raw = read_mode(rows32, m, modes, owned, halves)
        units = (raw * lax.rsqrt(jnp.sum(raw * raw, axis=-1, keepdims=True) + 1e-6)).astype(BF16)
        units_ref[rows, :] = units
        scores = lax.dot_general(units, unit_protos_ref[...], NT, preferred_element_type=F32)
        soft = jnp.exp(scores * 10.0)
        kernel = soft * soft
        kernel_ref[rows, :] = kernel.astype(BF16)
        soft_kernel_ref[rows, :] = soft.astype(BF16)
        line_to_tiles(mass_ref, m * (width // LANES), jnp.sum(kernel, axis=0, keepdims=True))
        folded = soft[:, :LANES]
        for j in range(1, width // LANES):
            folded = folded + soft[:, j * LANES : (j + 1) * LANES]
        high = folded.astype(BF16)
        low = (folded - high.astype(F32)).astype(BF16)
        ones = jnp.ones((16, LANES), BF16)
        line = lax.dot_general(ones, high, NT, preferred_element_type=F32)
        line = line + lax.dot_general(ones, low, NT, preferred_element_type=F32)
        lines.append(line[0:1])
    soft_ref[...] = lines_to_pair(lines)


def row_body(modes, mass_ref, kernel_ref, *refs):
    samples = kernel_ref.shape[0] // modes
    tiles = kernel_ref.shape[1] // LANES
    inverse = 1.0 / mass_ref[...]
    lines = []
    for m in range(modes):
        terms = two_terms(tiles_to_line(inverse, m * tiles, tiles))
        kernel = kernel_ref[m * samples : (m + 1) * samples, :]
        line = lax.dot_general(terms, kernel, NT, preferred_element_type=F32)
        lines.append(line[0:1] + line[1:2])
    pair = lines_to_pair(lines)
    if len(refs) == 1:
        refs[0][...] = pair
    else:
        soft_ref, row_ref, inverse_ref = refs
        row_ref[...] = jnp.concatenate([pair, soft_ref[...]], axis=0)
        inverse_ref[...] = inverse


def column_body(modes, row_ref, kernel_ref, mass_ref):
    samples = kernel_ref.shape[0] // modes
    width = kernel_ref.shape[1]
    weight = 1.0 / row_ref[...]
    for m in range(modes):
        terms = two_terms(mode_of(weight, m, samples // LANES))
        kernel = kernel_ref[m * samples : (m + 1) * samples, :]
        line = jnp.dot(terms, kernel, preferred_element_type=F32)
        line_to_tiles(mass_ref, m * (width // LANES), line[0:1] + line[1:2])


def upright_factors(totals_ref, width):
    return [
        jnp.concatenate([upright(factor)] * (width // LANES), axis=1)
        for factor in (COEFFICIENT / totals_ref[0:2], 2.0 * COEFFICIENT / totals_ref[2:4])
    ]


def all_but(values, m):
    return functools.reduce(jnp.add, [values[n] for n in range(len(values)) if n != m])


def unit_body(modes, owned, place_ref, totals_ref, inverse_ref, soft_ref, kernel_ref, unit_protos_ref, tied_ref, *refs):
    pieces, sums = refs[:-1], refs[-1]
    samples = kernel_ref.shape[0] // modes
    tiles = kernel_ref.shape[1] // LANES
    chunk = samples // owned // len(pieces)
    weight, spread = upright_factors(totals_ref, unit_protos_ref.shape[1])
    codes, predicted = [], []
    for m in range(modes):
        rows = slice(m * samples, (m + 1) * samples)
        inverse = tiles_to_line(inverse_ref[...], m * tiles, tiles)
        assigned = (kernel_ref[rows, :].astype(F32) * inverse).astype(BF16)
        codes.append(weight[rows] * jnp.dot(assigned, unit_protos_ref[...], preferred_element_type=F32))
        predicted.append(spread[rows] * jnp.dot(soft_ref[rows, :], unit_protos_ref[...], preferred_element_type=F32))
    for m in range(modes):
        sums[m * samples : (m + 1) * samples, :] = predicted[m] - all_but(codes, m)
    for step, piece in enumerate(pieces):
        place = lax.bitwise_xor(place_ref[0], jnp.int32(step)) * chunk
        for j in range(modes * owned):
            first = pl.multiple_of(place + j * (samples // owned), chunk)
            piece[j * chunk : (j + 1) * chunk, :] = sums[pl.ds(first, chunk), :].astype(BF16)


def proto_body(modes, totals_ref, inverse_ref, units_ref, soft_ref, kernel_ref, unit_protos_ref, proto_ref, mark_ref):
    mark_ref[...] = jnp.zeros_like(mark_ref)
    samples = units_ref.shape[0] // modes
    width = kernel_ref.shape[1]
    tiles = width // LANES
    weight, spread = upright_factors(totals_ref, units_ref.shape[1])
    units = [units_ref[m * samples : (m + 1) * samples, :].astype(F32) for m in range(modes)]
    rows = [slice(m * samples, (m + 1) * samples) for m in range(modes)]
    for_codes = [(weight[rows[m]] * all_but(units, m)).T.astype(BF16) for m in range(modes)]
    for_predicted = [(spread[rows[m]] * units[m]).T.astype(BF16) for m in range(modes)]
    step = 256
    for k in range(0, width, step):
        total = jnp.zeros((units_ref.shape[1], step), F32)
        for m in range(modes):
            inverse = tiles_to_line(inverse_ref[...], m * tiles + k // LANES, step // LANES)
            total = total + jnp.dot(for_predicted[m], soft_ref[rows[m], k : k + step], preferred_element_type=F32)
            total = total - inverse * jnp.dot(for_codes[m], kernel_ref[rows[m], k : k + step], preferred_element_type=F32)
        proto_ref[k : k + step, :] = total.T.astype(BF16)


def middle_body(parts_ref, share_ref, *refs):
    pieces, (grad_ref, rows_ref, unit) = refs[:-3], refs[-3:]
    total = jnp.sum(parts_ref[...].astype(F32), axis=0)
    raw = share_ref[...].astype(F32)
    scale = lax.rsqrt(jnp.sum(raw * raw, axis=-1, keepdims=True) + 1e-6)
    inner = jnp.sum(total * raw, axis=-1, keepdims=True)
    grad_ref[...] = (scale * total - scale * scale * scale * inner * raw).astype(BF16)
    total = functools.reduce(jnp.add, [piece[...].astype(F32) for piece in pieces])
    for h in range(unit.shape[0]):
        unit[h] = total[:, h * LANES : (h + 1) * LANES]
    cuts = rows_ref.shape[0]
    for j in range(cuts):
        rows_ref[j] = jnp.concatenate(
            [unit[h, pl.ds(j, unit.shape[1] // cuts, stride=cuts), :] for h in range(unit.shape[0])], axis=0
        ).astype(BF16)


def last_body(parts_ref, raw_ref, protos_ref, grad_ref, proto_grad_ref):
    proto_grad_ref[...] = protos_ref[...].astype(F32)
    total = jnp.sum(parts_ref[...].astype(F32), axis=0)
    raw = raw_ref[...].astype(F32)
    count = raw.shape[0]
    total = jnp.concatenate([total[h : h + count] for h in range(0, total.shape[0], count)], axis=1)
    scale = lax.rsqrt(jnp.sum(raw * raw, axis=-1, keepdims=True) + 1e-6)
    inner = jnp.sum(total * raw, axis=-1, keepdims=True)
    grad = scale * total - scale * scale * scale * inner * raw
    modes, owned = grad_ref.shape[:2]
    for m in range(modes):
        grad_ref[m] = grad[m * owned : (m + 1) * owned]


def exchange(x, axes):
    return lax.all_to_all(x, axes, 0, 0, tiled=True)


def copies(x, axes, count):
    return exchange(jnp.broadcast_to(x[None], (count,) + x.shape), axes)


def gather(x, axes, count):
    return copies(x, axes, count).reshape((count * x.shape[0],) + x.shape[1:])


def sum_over(x, axes, count):
    return jnp.sum(copies(x.astype(BF16), axes, count).astype(F32), axis=0)


def swap(x, axis, count, step):
    return lax.ppermute(x, axis, [(i, i ^ step) for i in range(count)]) if step else x


def per_device(sizes, embeddings, prototypes):
    modes, width = embeddings.shape[1:]
    own_samples = embeddings.shape[0]
    owned = own_samples * modes
    local_protos = prototypes.shape[0]
    ny, nc, nx, nz = (sizes[a] for a in ("y", "core", "x", "z"))
    dp = ("y", "core")
    groups = ny * nc
    lines = owned * nx * nz
    x_lines = lines // nx
    mass_shape = shape((modes * local_protos // LANES, LANES), F32)
    row_shape = shape((2, lines // 2), F32)
    units_shape = shape((lines, width), BF16)
    dp_place = lax.axis_index(dp).reshape(1)
    x_place = lax.axis_index("x").reshape(1)

    row_call = call(functools.partial(row_body, modes), "row_sum", row_shape, [WHOLE] * 2)
    last_row_call = call(
        functools.partial(row_body, modes), "row_sum", [shape((4, lines // 2), F32), mass_shape], [WHOLE] * 3
    )
    column_call = call(functools.partial(column_body, modes), "column_sum", mass_shape, [WHOLE] * 2)

    raw_rows = embeddings.transpose(1, 0, 2).reshape(owned, width)
    raw_tiles = jnp.concatenate([raw_rows[:, h : h + LANES] for h in range(0, width, LANES)], axis=0)
    gathered = gather(gather(raw_tiles, "z", nz), "x", nx)
    kernel, soft_kernel, units, unit_protos, soft, mass, own_share = call(
        functools.partial(score_body, modes, own_samples),
        "scores",
        [shape((lines, local_protos), BF16)] * 2
        + [units_shape, shape((local_protos, width), BF16), row_shape, mass_shape, shape((local_protos // groups, width), BF16)],
        [SCALARS] + [WHOLE] * 2,
        [pltpu.VMEM(gathered.shape, F32)],
    )(dp_place, gathered, prototypes)

    for _ in range(2):
        row = row_call(sum_over(mass, dp, groups), kernel)
        mass = column_call(sum_over(row, ("x", "z"), nx * nz), kernel)
    row, inverse = last_row_call(sum_over(mass, dp, groups), kernel, soft)
    totals = sum_over(row, ("x", "z"), nx * nz)

    proto_part, mark = call(
        functools.partial(proto_body, modes),
        "proto_part",
        [shape((local_protos, width), BF16), shape((8, LANES), F32)],
        [WHOLE] * 6,
    )(totals, inverse, units, soft_kernel, kernel, unit_protos)
    pieces = call(
        functools.partial(unit_body, modes, own_samples),
        "unit_grad",
        [shape((x_lines, width), BF16)] * nx,
        [SCALARS] + [WHOLE] * 6,
        [pltpu.VMEM((lines, width), F32)],
    )(x_place, totals, inverse, soft_kernel, kernel, unit_protos, mark)
    proto_part = exchange(proto_part, dp).reshape(groups, local_protos // groups, width)
    pieces = [pieces[0]] + [swap(pieces[step], "x", nx, step) for step in (2, 1, 3)]
    proto_grad, rows = call(
        middle_body,
        "middle",
        [shape((local_protos // groups, width), BF16), shape((nz, owned * width // LANES, LANES), BF16)],
        [WHOLE] * (2 + nx),
        [pltpu.VMEM((width // LANES, x_lines, LANES), F32)],
    )(proto_part, own_share, *pieces)
    rows = exchange(rows, "z")
    proto_grad = lax.all_gather(proto_grad, dp, axis=0, tiled=True)
    embed_grad, proto_grad = call(
        last_body,
        "last",
        [shape((modes, own_samples, width), F32), shape((local_protos, width), F32)],
        [WHOLE] * 3,
    )(rows, raw_rows, proto_grad)
    return (embed_grad.transpose(1, 0, 2), proto_grad)


def solution(mesh):
    sizes = dict(y=mesh.shape["dp"] // 2, core=2, x=4, z=mesh.shape["proto"] // 4)
    fine = Mesh(mesh.devices.reshape(tuple(sizes.values())), tuple(sizes))
    specs = (P(("y", "core", "x", "z"), None, None), P(("x", "z"), None))
    return jax.shard_map(
        functools.partial(per_device, sizes), mesh=fine, in_specs=specs, out_specs=specs, check_vma=False
    )
```

```python
import functools

import jax
import jax.numpy as jnp
from jax import lax
from jax.experimental import pallas as pl
from jax.experimental.pallas import tpu as pltpu
from jax.sharding import Mesh, PartitionSpec as P

F32 = jnp.float32
BF16 = jnp.bfloat16
LANES = 128
COEFFICIENT = 64.0 * 10.0 / 6.0
LOG2_E = 1.4426950408889634
NT = (((1,), (1,)), ((), ()))
SCALARS = pl.BlockSpec(memory_space=pltpu.SMEM)
WHOLE = pl.BlockSpec(memory_space=pltpu.VMEM)
ANYWHERE = pl.BlockSpec(memory_space=pl.ANY)


def call(body, name, out_shapes, in_specs, scratch=(), out_specs=None, aliases=None):
    many = isinstance(out_shapes, (list, tuple))
    return pl.pallas_call(
        body,
        name=name,
        in_specs=in_specs,
        out_shape=out_shapes,
        out_specs=out_specs or ([WHOLE] * len(out_shapes) if many else WHOLE),
        scratch_shapes=list(scratch),
        input_output_aliases=aliases or {},
        compiler_params=pltpu.CompilerParams(vmem_limit_bytes=28 * 1024 * 1024),
    )


def shape(dims, dtype):
    return jax.ShapeDtypeStruct(dims, dtype)


def tiles_to_line(block, first, count):
    return jnp.concatenate([block[first + j : first + j + 1] for j in range(count)], axis=1)


def line_to_tiles(ref, first, line):
    for j in range(line.shape[1] // LANES):
        ref[first + j : first + j + 1, :] = line[:, j * LANES : (j + 1) * LANES]


def tile_of(pair, tile):
    half = pair.shape[1] // LANES
    return pair[tile // half : tile // half + 1, (tile % half) * LANES : (tile % half + 1) * LANES]


def mode_of(pair, m, tiles):
    return jnp.concatenate([tile_of(pair, m * tiles + j) for j in range(tiles)], axis=1)


def lines_to_pair(lines):
    whole = jnp.concatenate(lines, axis=1)
    half = whole.shape[1] // 2
    return jnp.concatenate([whole[:, :half], whole[:, half:]], axis=0)


def upright(pair):
    count = 2 * pair.shape[1] // LANES
    block = jnp.concatenate([tile_of(pair, t) for t in range(count)] + [tile_of(pair, 0)] * (-count % 8), axis=0).T
    return jnp.concatenate([jnp.broadcast_to(block[:, t : t + 1], (LANES, LANES)) for t in range(count)], axis=0)


def two_terms(line):
    high = line.astype(BF16).astype(F32)
    row = lax.broadcasted_iota(jnp.int32, (16, line.shape[1]), 0)
    return jnp.where(row == 0, high, jnp.where(row == 1, line - high, 0.0)).astype(BF16)


def read_mode(ref, m, modes, owned, halves):
    per_owner = halves * modes * owned
    count = ref.shape[0] // per_owner
    parts = [
        jnp.concatenate(
            [ref[pl.ds((h * modes + m) * owned + i, count, stride=per_owner), :] for h in range(halves)], axis=1
        )
        for i in range(owned)
    ]
    return jnp.concatenate(parts, axis=0)


def score_body(modes, owned, rows_ref, protos_ref, kernel_ref, units_ref, unit_protos_ref, soft_ref, mass_ref, rows32):
    samples = units_ref.shape[0] // modes
    width = protos_ref.shape[0]
    halves = protos_ref.shape[1] // LANES
    raw = protos_ref[...].astype(F32)
    scale = lax.rsqrt(jnp.sum(raw * raw, axis=-1, keepdims=True) + 1e-6)
    unit_protos_ref[...] = (raw * scale).astype(BF16)
    rows32[...] = rows_ref[...].astype(F32)
    lines = []
    for m in range(modes):
        rows = slice(m * samples, (m + 1) * samples)
        raw = read_mode(rows32, m, modes, owned, halves)
        units = (raw * lax.rsqrt(jnp.sum(raw * raw, axis=-1, keepdims=True) + 1e-6)).astype(BF16)
        units_ref[rows, :] = units
        scores = lax.dot_general(units, unit_protos_ref[...], NT, preferred_element_type=F32)
        soft = jnp.exp2(scores * (10.0 * LOG2_E))
        kernel = soft * soft
        kernel_ref[rows, :] = kernel.astype(BF16)
        line_to_tiles(mass_ref, m * (width // LANES), jnp.sum(kernel, axis=0, keepdims=True))
        folded = soft[:, :LANES]
        for j in range(1, width // LANES):
            folded = folded + soft[:, j * LANES : (j + 1) * LANES]
        high = folded.astype(BF16)
        low = (folded - high.astype(F32)).astype(BF16)
        ones = jnp.ones((16, LANES), BF16)
        line = lax.dot_general(ones, high, NT, preferred_element_type=F32)
        line = line + lax.dot_general(ones, low, NT, preferred_element_type=F32)
        lines.append(line[0:1])
    soft_ref[...] = lines_to_pair(lines)


def row_body(modes, mass_ref, kernel_ref, *refs):
    samples = kernel_ref.shape[0] // modes
    tiles = kernel_ref.shape[1] // LANES
    inverse = 1.0 / mass_ref[...]
    lines = []
    for m in range(modes):
        terms = two_terms(tiles_to_line(inverse, m * tiles, tiles))
        kernel = kernel_ref[m * samples : (m + 1) * samples, :]
        line = lax.dot_general(terms, kernel, NT, preferred_element_type=F32)
        lines.append(line[0:1] + line[1:2])
    pair = lines_to_pair(lines)
    if len(refs) == 1:
        refs[0][...] = pair
    else:
        soft_ref, row_ref, inverse_ref = refs
        row_ref[...] = jnp.concatenate([pair, soft_ref[...]], axis=0)
        inverse_ref[...] = inverse


def column_body(modes, row_ref, kernel_ref, mass_ref):
    samples = kernel_ref.shape[0] // modes
    width = kernel_ref.shape[1]
    weight = 1.0 / row_ref[...]
    for m in range(modes):
        terms = two_terms(mode_of(weight, m, samples // LANES))
        kernel = kernel_ref[m * samples : (m + 1) * samples, :]
        line = jnp.dot(terms, kernel, preferred_element_type=F32)
        line_to_tiles(mass_ref, m * (width // LANES), line[0:1] + line[1:2])


def unit_body(modes, owned, place_ref, totals_ref, inverse_ref, units_ref, unit_protos_ref, tied_ref, *refs):
    pieces, (weights, sums) = refs[:-2], refs[-2:]
    samples = units_ref.shape[0] // modes
    width = unit_protos_ref.shape[0]
    tiles = width // LANES
    chunk = samples // owned // len(pieces)
    weights[0] = upright(COEFFICIENT / totals_ref[0:2])
    weights[1] = upright(2.0 * COEFFICIENT / totals_ref[2:4])
    step = 512
    for k in range(0, width, step):
        protos = unit_protos_ref[k : k + step, :]
        scores = lax.dot_general(units_ref[...], protos, NT, preferred_element_type=F32)
        codes, predicted = [], []
        for m in range(modes):
            rows = slice(m * samples, (m + 1) * samples)
            soft = jnp.exp2((10.0 * LOG2_E) * scores[rows])
            inverse = tiles_to_line(inverse_ref[...], m * tiles + k // LANES, step // LANES)
            codes.append(soft * soft * inverse * jnp.concatenate([weights[0, rows, :]] * (step // LANES), axis=1))
            predicted.append(soft * jnp.concatenate([weights[1, rows, :]] * (step // LANES), axis=1))
        for m in range(modes):
            rows = slice(m * samples, (m + 1) * samples)
            logit = predicted[m] - functools.reduce(jnp.add, [codes[n] for n in range(modes) if n != m])
            part = jnp.dot(logit.astype(BF16), protos, preferred_element_type=F32)
            sums[rows, :] = part if k == 0 else sums[rows, :] + part
    for step, piece in enumerate(pieces):
        place = lax.bitwise_xor(place_ref[0], jnp.int32(step)) * chunk
        for j in range(modes * owned):
            first = pl.multiple_of(place + j * (samples // owned), chunk)
            piece[j * chunk : (j + 1) * chunk, :] = sums[pl.ds(first, chunk), :].astype(BF16)


def proto_body(modes, totals_ref, inverse_ref, units_ref, unit_protos_ref, proto_ref):
    samples = units_ref.shape[0] // modes
    width = unit_protos_ref.shape[0]
    tiles = width // LANES
    inverse = inverse_ref[...].T
    weight = COEFFICIENT / totals_ref[0:2]
    spread = 2.0 * COEFFICIENT / totals_ref[2:4]
    weight = [mode_of(weight, m, samples // LANES) for m in range(modes)]
    spread = [mode_of(spread, m, samples // LANES) for m in range(modes)]
    step = 256
    for k in range(0, width, step):
        scores = lax.dot_general(unit_protos_ref[k : k + step, :], units_ref[...], NT, preferred_element_type=F32)
        codes, predicted = [], []
        for m in range(modes):
            first = m * tiles + k // LANES
            upright_inverse = jnp.concatenate([inverse[:, first + j : first + j + 1] for j in range(step // LANES)], axis=0)
            soft = jnp.exp2((10.0 * LOG2_E) * scores[:, m * samples : (m + 1) * samples])
            codes.append(soft * soft * upright_inverse * weight[m])
            predicted.append(soft * spread[m])
        logit = [
            (predicted[m] - functools.reduce(jnp.add, [codes[n] for n in range(modes) if n != m])).astype(BF16)
            for m in range(modes)
        ]
        proto_ref[k : k + step, :] = jnp.dot(
            jnp.concatenate(logit, axis=1), units_ref[...], preferred_element_type=F32
        ).astype(BF16)


def middle_body(place_ref, parts_ref, protos_ref, *refs):
    pieces, (grad_ref, rows_ref, unit) = refs[:-3], refs[-3:]
    total = jnp.sum(parts_ref[...].astype(F32), axis=0)
    share = total.shape[0]
    raw = protos_ref[pl.ds(pl.multiple_of(place_ref[0] * share, share), share), :].astype(F32)
    scale = lax.rsqrt(jnp.sum(raw * raw, axis=-1, keepdims=True) + 1e-6)
    inner = jnp.sum(total * raw, axis=-1, keepdims=True)
    grad_ref[...] = (scale * total - scale * scale * scale * inner * raw).astype(BF16)
    total = functools.reduce(jnp.add, [piece[...].astype(F32) for piece in pieces])
    for h in range(unit.shape[0]):
        unit[h] = total[:, h * LANES : (h + 1) * LANES]
    cuts = rows_ref.shape[0]
    for j in range(cuts):
        rows_ref[j] = jnp.concatenate(
            [unit[h, pl.ds(j, unit.shape[1] // cuts, stride=cuts), :] for h in range(unit.shape[0])], axis=0
        ).astype(BF16)


def last_body(parts_ref, raw_ref, protos_ref, grad_ref, proto_grad_ref):
    proto_grad_ref[...] = protos_ref[...].astype(F32)
    total = jnp.sum(parts_ref[...].astype(F32), axis=0)
    raw = raw_ref[...].astype(F32)
    count = raw.shape[0]
    total = jnp.concatenate([total[h : h + count] for h in range(0, total.shape[0], count)], axis=1)
    scale = lax.rsqrt(jnp.sum(raw * raw, axis=-1, keepdims=True) + 1e-6)
    inner = jnp.sum(total * raw, axis=-1, keepdims=True)
    grad = scale * total - scale * scale * scale * inner * raw
    modes, owned = grad_ref.shape[:2]
    for m in range(modes):
        grad_ref[m] = grad[m * owned : (m + 1) * owned]


def exchange(x, axes):
    return lax.all_to_all(x, axes, 0, 0, tiled=True)


def copies(x, axes, count):
    return exchange(jnp.broadcast_to(x[None], (count,) + x.shape), axes)


def gather(x, axes, count):
    return copies(x, axes, count).reshape((count * x.shape[0],) + x.shape[1:])


def sum_over(x, axes, count):
    return jnp.sum(copies(x.astype(BF16), axes, count).astype(F32), axis=0)


def swap(x, axis, count, step):
    return lax.ppermute(x, axis, [(i, i ^ step) for i in range(count)]) if step else x


def per_device(sizes, embeddings, prototypes):
    modes, width = embeddings.shape[1:]
    own_samples = embeddings.shape[0]
    owned = own_samples * modes
    local_protos = prototypes.shape[0]
    ny, nc, nx, nz = (sizes[a] for a in ("y", "core", "x", "z"))
    dp = ("y", "core")
    groups = ny * nc
    lines = owned * nx * nz
    x_lines = lines // nx
    mass_shape = shape((modes * local_protos // LANES, LANES), F32)
    row_shape = shape((2, lines // 2), F32)
    units_shape = shape((lines, width), BF16)
    dp_place = lax.axis_index(dp).reshape(1)
    x_place = lax.axis_index("x").reshape(1)

    row_call = call(functools.partial(row_body, modes), "row_sum", row_shape, [WHOLE] * 2)
    last_row_call = call(
        functools.partial(row_body, modes), "row_sum", [shape((4, lines // 2), F32), mass_shape], [WHOLE] * 3
    )
    column_call = call(functools.partial(column_body, modes), "column_sum", mass_shape, [WHOLE] * 2)

    raw_rows = embeddings.transpose(1, 0, 2).reshape(owned, width)
    raw_tiles = jnp.concatenate([raw_rows[:, h : h + LANES] for h in range(0, width, LANES)], axis=0)
    gathered = gather(gather(raw_tiles, "z", nz), "x", nx)
    kernel, units, unit_protos, soft, mass = call(
        functools.partial(score_body, modes, own_samples),
        "scores",
        [shape((lines, local_protos), BF16), units_shape, shape((local_protos, width), BF16), row_shape, mass_shape],
        [WHOLE] * 2,
        [pltpu.VMEM(gathered.shape, F32)],
    )(gathered, prototypes)

    for _ in range(2):
        row = row_call(sum_over(mass, dp, groups), kernel)
        mass = column_call(sum_over(row, ("x", "z"), nx * nz), kernel)
    row, inverse = last_row_call(sum_over(mass, dp, groups), kernel, soft)
    totals = sum_over(row, ("x", "z"), nx * nz)

    proto_part = call(
        functools.partial(proto_body, modes), "proto_part", shape((local_protos, width), BF16), [WHOLE] * 4
    )(totals, inverse, units, unit_protos)
    pieces = call(
        functools.partial(unit_body, modes, own_samples),
        "unit_grad",
        [shape((x_lines, width), BF16)] * nx,
        [SCALARS] + [WHOLE] * 4 + [ANYWHERE],
        [pltpu.VMEM((2, lines, LANES), F32), pltpu.VMEM((lines, width), F32)],
    )(x_place, totals, inverse, units, unit_protos, proto_part)
    proto_part = exchange(proto_part, dp).reshape(groups, local_protos // groups, width)
    pieces = [pieces[0]] + [swap(pieces[step], "x", nx, step) for step in (2, 1, 3)]
    proto_grad, rows = call(
        middle_body,
        "middle",
        [shape((local_protos // groups, width), BF16), shape((nz, owned * width // LANES, LANES), BF16)],
        [SCALARS] + [WHOLE] * (2 + nx),
        [pltpu.VMEM((width // LANES, x_lines, LANES), F32)],
    )(dp_place, proto_part, prototypes, *pieces)
    rows = exchange(rows, "z")
    proto_grad = lax.all_gather(proto_grad, dp, axis=0, tiled=True)
    embed_grad, proto_grad = call(
        last_body,
        "last",
        [shape((modes, own_samples, width), F32), shape((local_protos, width), F32)],
        [WHOLE] * 3,
    )(rows, raw_rows, proto_grad)
    return (embed_grad.transpose(1, 0, 2), proto_grad)


def solution(mesh):
    sizes = dict(y=mesh.shape["dp"] // 2, core=2, x=4, z=mesh.shape["proto"] // 4)
    fine = Mesh(mesh.devices.reshape(tuple(sizes.values())), tuple(sizes))
    specs = (P(("y", "core", "x", "z"), None, None), P(("x", "z"), None))
    return jax.shard_map(
        functools.partial(per_device, sizes), mesh=fine, in_specs=specs, out_specs=specs, check_vma=False
    )
```

```python
import functools

import jax
import jax.numpy as jnp
from jax import lax
from jax.experimental import pallas as pl
from jax.experimental.pallas import tpu as pltpu
from jax.sharding import Mesh, PartitionSpec as P

F32 = jnp.float32
BF16 = jnp.bfloat16
LANES = 128
COEFFICIENT = 64.0 * 10.0 / 6.0
LOG2_E = 1.4426950408889634
NT = (((1,), (1,)), ((), ()))
SCALARS = pl.BlockSpec(memory_space=pltpu.SMEM)
WHOLE = pl.BlockSpec(memory_space=pltpu.VMEM)
ANYWHERE = pl.BlockSpec(memory_space=pl.ANY)


def call(body, name, out_shapes, in_specs, scratch=(), out_specs=None, aliases=None):
    many = isinstance(out_shapes, (list, tuple))
    return pl.pallas_call(
        body,
        name=name,
        in_specs=in_specs,
        out_shape=out_shapes,
        out_specs=out_specs or ([WHOLE] * len(out_shapes) if many else WHOLE),
        scratch_shapes=list(scratch),
        input_output_aliases=aliases or {},
        compiler_params=pltpu.CompilerParams(vmem_limit_bytes=28 * 1024 * 1024),
    )


def shape(dims, dtype):
    return jax.ShapeDtypeStruct(dims, dtype)


def tiles_to_line(block, first, count):
    return jnp.concatenate([block[first + j : first + j + 1] for j in range(count)], axis=1)


def line_to_tiles(ref, first, line):
    for j in range(line.shape[1] // LANES):
        ref[first + j : first + j + 1, :] = line[:, j * LANES : (j + 1) * LANES]


def tile_of(pair, tile):
    half = pair.shape[1] // LANES
    return pair[tile // half : tile // half + 1, (tile % half) * LANES : (tile % half + 1) * LANES]


def mode_of(pair, m, tiles):
    return jnp.concatenate([tile_of(pair, m * tiles + j) for j in range(tiles)], axis=1)


def lines_to_pair(lines):
    whole = jnp.concatenate(lines, axis=1)
    half = whole.shape[1] // 2
    return jnp.concatenate([whole[:, :half], whole[:, half:]], axis=0)


def upright(pair):
    count = 2 * pair.shape[1] // LANES
    block = jnp.concatenate([tile_of(pair, t) for t in range(count)] + [tile_of(pair, 0)] * (-count % 8), axis=0).T
    return jnp.concatenate([jnp.broadcast_to(block[:, t : t + 1], (LANES, LANES)) for t in range(count)], axis=0)


def two_terms(line):
    high = line.astype(BF16).astype(F32)
    row = lax.broadcasted_iota(jnp.int32, (16, line.shape[1]), 0)
    return jnp.where(row == 0, high, jnp.where(row == 1, line - high, 0.0)).astype(BF16)


def read_mode(ref, m, modes, owned, halves):
    per_owner = halves * modes * owned
    count = ref.shape[0] // per_owner
    parts = [
        jnp.concatenate(
            [ref[pl.ds((h * modes + m) * owned + i, count, stride=per_owner), :] for h in range(halves)], axis=1
        )
        for i in range(owned)
    ]
    return jnp.concatenate(parts, axis=0)


def score_body(modes, owned, rows_ref, protos_ref, kernel_ref, units_ref, unit_protos_ref, soft_ref, mass_ref, rows32):
    samples = units_ref.shape[0] // modes
    width = protos_ref.shape[0]
    halves = protos_ref.shape[1] // LANES
    raw = protos_ref[...].astype(F32)
    scale = lax.rsqrt(jnp.sum(raw * raw, axis=-1, keepdims=True) + 1e-6)
    unit_protos_ref[...] = (raw * scale).astype(BF16)
    rows32[...] = rows_ref[...].astype(F32)
    lines = []
    for m in range(modes):
        rows = slice(m * samples, (m + 1) * samples)
        raw = read_mode(rows32, m, modes, owned, halves)
        units = (raw * lax.rsqrt(jnp.sum(raw * raw, axis=-1, keepdims=True) + 1e-6)).astype(BF16)
        units_ref[rows, :] = units
        scores = lax.dot_general(units, unit_protos_ref[...], NT, preferred_element_type=F32)
        soft = jnp.exp2(scores * (10.0 * LOG2_E))
        kernel = soft * soft
        kernel_ref[rows, :] = kernel.astype(BF16)
        line_to_tiles(mass_ref, m * (width // LANES), jnp.sum(kernel, axis=0, keepdims=True))
        folded = soft[:, :LANES]
        for j in range(1, width // LANES):
            folded = folded + soft[:, j * LANES : (j + 1) * LANES]
        high = folded.astype(BF16)
        low = (folded - high.astype(F32)).astype(BF16)
        ones = jnp.ones((16, LANES), BF16)
        line = lax.dot_general(ones, high, NT, preferred_element_type=F32)
        line = line + lax.dot_general(ones, low, NT, preferred_element_type=F32)
        lines.append(line[0:1])
    soft_ref[...] = lines_to_pair(lines)


def row_body(modes, mass_ref, kernel_ref, *refs):
    samples = kernel_ref.shape[0] // modes
    tiles = kernel_ref.shape[1] // LANES
    inverse = 1.0 / mass_ref[...]
    lines = []
    for m in range(modes):
        terms = two_terms(tiles_to_line(inverse, m * tiles, tiles))
        kernel = kernel_ref[m * samples : (m + 1) * samples, :]
        line = lax.dot_general(terms, kernel, NT, preferred_element_type=F32)
        lines.append(line[0:1] + line[1:2])
    pair = lines_to_pair(lines)
    if len(refs) == 1:
        refs[0][...] = pair
    else:
        soft_ref, row_ref, inverse_ref = refs
        row_ref[...] = jnp.concatenate([pair, soft_ref[...]], axis=0)
        inverse_ref[...] = inverse


def column_body(modes, row_ref, kernel_ref, mass_ref):
    samples = kernel_ref.shape[0] // modes
    width = kernel_ref.shape[1]
    weight = 1.0 / row_ref[...]
    for m in range(modes):
        terms = two_terms(mode_of(weight, m, samples // LANES))
        kernel = kernel_ref[m * samples : (m + 1) * samples, :]
        line = jnp.dot(terms, kernel, preferred_element_type=F32)
        line_to_tiles(mass_ref, m * (width // LANES), line[0:1] + line[1:2])


def unit_body(modes, owned, place_ref, totals_ref, inverse_ref, units_ref, unit_protos_ref, tied_ref, *refs):
    pieces, (weights, sums) = refs[:-2], refs[-2:]
    samples = units_ref.shape[0] // modes
    width = unit_protos_ref.shape[0]
    tiles = width // LANES
    chunk = samples // owned // len(pieces)
    weights[0] = upright(COEFFICIENT / totals_ref[0:2])
    weights[1] = upright(2.0 * COEFFICIENT / totals_ref[2:4])
    step = 512
    for k in range(0, width, step):
        protos = unit_protos_ref[k : k + step, :]
        scores = lax.dot_general(units_ref[...], protos, NT, preferred_element_type=F32)
        codes, predicted = [], []
        for m in range(modes):
            rows = slice(m * samples, (m + 1) * samples)
            soft = jnp.exp2((10.0 * LOG2_E) * scores[rows])
            inverse = tiles_to_line(inverse_ref[...], m * tiles + k // LANES, step // LANES)
            codes.append(soft * soft * inverse * jnp.concatenate([weights[0, rows, :]] * (step // LANES), axis=1))
            predicted.append(soft * jnp.concatenate([weights[1, rows, :]] * (step // LANES), axis=1))
        for m in range(modes):
            rows = slice(m * samples, (m + 1) * samples)
            logit = predicted[m] - functools.reduce(jnp.add, [codes[n] for n in range(modes) if n != m])
            part = jnp.dot(logit.astype(BF16), protos, preferred_element_type=F32)
            sums[rows, :] = part if k == 0 else sums[rows, :] + part
    for step, piece in enumerate(pieces):
        place = lax.bitwise_xor(place_ref[0], jnp.int32(step)) * chunk
        for j in range(modes * owned):
            first = pl.multiple_of(place + j * (samples // owned), chunk)
            piece[j * chunk : (j + 1) * chunk, :] = sums[pl.ds(first, chunk), :].astype(BF16)


def proto_body(modes, totals_ref, inverse_ref, units_ref, unit_protos_ref, proto_ref):
    samples = units_ref.shape[0] // modes
    width = unit_protos_ref.shape[0]
    tiles = width // LANES
    inverse = inverse_ref[...].T
    weight = COEFFICIENT / totals_ref[0:2]
    spread = 2.0 * COEFFICIENT / totals_ref[2:4]
    weight = [mode_of(weight, m, samples // LANES) for m in range(modes)]
    spread = [mode_of(spread, m, samples // LANES) for m in range(modes)]
    step = 256
    for k in range(0, width, step):
        scores = lax.dot_general(unit_protos_ref[k : k + step, :], units_ref[...], NT, preferred_element_type=F32)
        codes, predicted = [], []
        for m in range(modes):
            first = m * tiles + k // LANES
            upright_inverse = jnp.concatenate([inverse[:, first + j : first + j + 1] for j in range(step // LANES)], axis=0)
            soft = jnp.exp2((10.0 * LOG2_E) * scores[:, m * samples : (m + 1) * samples])
            codes.append(soft * soft * upright_inverse * weight[m])
            predicted.append(soft * spread[m])
        logit = [
            (predicted[m] - functools.reduce(jnp.add, [codes[n] for n in range(modes) if n != m])).astype(BF16)
            for m in range(modes)
        ]
        proto_ref[k : k + step, :] = jnp.dot(
            jnp.concatenate(logit, axis=1), units_ref[...], preferred_element_type=F32
        ).astype(BF16)


def middle_body(place_ref, parts_ref, protos_ref, *refs):
    pieces, (grad_ref, rows_ref, unit) = refs[:-3], refs[-3:]
    total = jnp.sum(parts_ref[...].astype(F32), axis=0)
    share = total.shape[0]
    raw = protos_ref[pl.ds(pl.multiple_of(place_ref[0] * share, share), share), :].astype(F32)
    scale = lax.rsqrt(jnp.sum(raw * raw, axis=-1, keepdims=True) + 1e-6)
    inner = jnp.sum(total * raw, axis=-1, keepdims=True)
    grad_ref[...] = (scale * total - scale * scale * scale * inner * raw).astype(BF16)
    total = functools.reduce(jnp.add, [piece[...].astype(F32) for piece in pieces])
    for h in range(unit.shape[0]):
        unit[h] = total[:, h * LANES : (h + 1) * LANES]
    cuts = rows_ref.shape[0]
    for j in range(cuts):
        rows_ref[j] = jnp.concatenate(
            [unit[h, pl.ds(j, unit.shape[1] // cuts, stride=cuts), :] for h in range(unit.shape[0])], axis=0
        ).astype(BF16)


def last_body(parts_ref, raw_ref, protos_ref, grad_ref, proto_grad_ref):
    proto_grad_ref[...] = protos_ref[...].astype(F32)
    total = jnp.sum(parts_ref[...].astype(F32), axis=0)
    raw = raw_ref[...].astype(F32)
    count = raw.shape[0]
    total = jnp.concatenate([total[h : h + count] for h in range(0, total.shape[0], count)], axis=1)
    scale = lax.rsqrt(jnp.sum(raw * raw, axis=-1, keepdims=True) + 1e-6)
    inner = jnp.sum(total * raw, axis=-1, keepdims=True)
    grad = scale * total - scale * scale * scale * inner * raw
    modes, owned = grad_ref.shape[:2]
    for m in range(modes):
        grad_ref[m] = grad[m * owned : (m + 1) * owned]


def exchange(x, axes):
    return lax.all_to_all(x, axes, 0, 0, tiled=True)


def copies(x, axes, count):
    return exchange(jnp.broadcast_to(x[None], (count,) + x.shape), axes)


def gather(x, axes, count):
    return copies(x, axes, count).reshape((count * x.shape[0],) + x.shape[1:])


def sum_over(x, axes, count):
    return jnp.sum(copies(x.astype(BF16), axes, count).astype(F32), axis=0)


def swap(x, axis, count, step):
    return lax.ppermute(x, axis, [(i, i ^ step) for i in range(count)]) if step else x


def per_device(sizes, embeddings, prototypes):
    modes, width = embeddings.shape[1:]
    own_samples = embeddings.shape[0]
    owned = own_samples * modes
    local_protos = prototypes.shape[0]
    ny, nc, nx, nz = (sizes[a] for a in ("y", "core", "x", "z"))
    dp = ("y", "core")
    groups = ny * nc
    lines = owned * nx * nz
    x_lines = lines // nx
    mass_shape = shape((modes * local_protos // LANES, LANES), F32)
    row_shape = shape((2, lines // 2), F32)
    units_shape = shape((lines, width), BF16)
    dp_place = lax.axis_index(dp).reshape(1)
    x_place = lax.axis_index("x").reshape(1)

    row_call = call(functools.partial(row_body, modes), "row_sum", row_shape, [WHOLE] * 2)
    last_row_call = call(
        functools.partial(row_body, modes), "row_sum", [shape((4, lines // 2), F32), mass_shape], [WHOLE] * 3
    )
    column_call = call(functools.partial(column_body, modes), "column_sum", mass_shape, [WHOLE] * 2)

    raw_rows = embeddings.transpose(1, 0, 2).reshape(owned, width)
    raw_tiles = jnp.concatenate([raw_rows[:, h : h + LANES] for h in range(0, width, LANES)], axis=0)
    gathered = gather(gather(raw_tiles, "z", nz), "x", nx)
    kernel, units, unit_protos, soft, mass = call(
        functools.partial(score_body, modes, own_samples),
        "scores",
        [shape((lines, local_protos), BF16), units_shape, shape((local_protos, width), BF16), row_shape, mass_shape],
        [WHOLE] * 2,
        [pltpu.VMEM(gathered.shape, F32)],
    )(gathered, prototypes)

    for _ in range(2):
        row = row_call(sum_over(mass, ("core", "y"), groups), kernel)
        mass = column_call(sum_over(row, ("z", "x"), nx * nz), kernel)
    row, inverse = last_row_call(sum_over(mass, ("core", "y"), groups), kernel, soft)
    totals = sum_over(row, ("z", "x"), nx * nz)

    proto_part = call(
        functools.partial(proto_body, modes), "proto_part", shape((local_protos, width), BF16), [WHOLE] * 4
    )(totals, inverse, units, unit_protos)
    pieces = call(
        functools.partial(unit_body, modes, own_samples),
        "unit_grad",
        [shape((x_lines, width), BF16)] * nx,
        [SCALARS] + [WHOLE] * 4 + [ANYWHERE],
        [pltpu.VMEM((2, lines, LANES), F32), pltpu.VMEM((lines, width), F32)],
    )(x_place, totals, inverse, units, unit_protos, proto_part)
    proto_part = exchange(proto_part, dp).reshape(groups, local_protos // groups, width)
    pieces = [pieces[0]] + [swap(pieces[step], "x", nx, step) for step in (2, 1, 3)]
    proto_grad, rows = call(
        middle_body,
        "middle",
        [shape((local_protos // groups, width), BF16), shape((nz, owned * width // LANES, LANES), BF16)],
        [SCALARS] + [WHOLE] * (2 + nx),
        [pltpu.VMEM((width // LANES, x_lines, LANES), F32)],
    )(dp_place, proto_part, prototypes, *pieces)
    rows = exchange(rows, "z")
    proto_grad = lax.all_gather(proto_grad, dp, axis=0, tiled=True)
    embed_grad, proto_grad = call(
        last_body,
        "last",
        [shape((modes, own_samples, width), F32), shape((local_protos, width), F32)],
        [WHOLE] * 3,
    )(rows, raw_rows, proto_grad)
    return (embed_grad.transpose(1, 0, 2), proto_grad)


def solution(mesh):
    sizes = dict(y=mesh.shape["dp"] // 2, core=2, x=4, z=mesh.shape["proto"] // 4)
    fine = Mesh(mesh.devices.reshape(tuple(sizes.values())), tuple(sizes))
    specs = (P(("y", "core", "x", "z"), None, None), P(("x", "z"), None))
    return jax.shard_map(
        functools.partial(per_device, sizes), mesh=fine, in_specs=specs, out_specs=specs, check_vma=False
    )
```

```python
import functools

import jax
import jax.numpy as jnp
from jax import lax
from jax.experimental import pallas as pl
from jax.experimental.pallas import tpu as pltpu
from jax.sharding import Mesh, PartitionSpec as P

F32 = jnp.float32
BF16 = jnp.bfloat16
LANES = 128
COEFFICIENT = 64.0 * 10.0 / 6.0
LOG2_E = 1.4426950408889634
NT = (((1,), (1,)), ((), ()))
SCALARS = pl.BlockSpec(memory_space=pltpu.SMEM)
WHOLE = pl.BlockSpec(memory_space=pltpu.VMEM)
ANYWHERE = pl.BlockSpec(memory_space=pl.ANY)


def call(body, name, out_shapes, in_specs, scratch=(), out_specs=None, aliases=None):
    many = isinstance(out_shapes, (list, tuple))
    return pl.pallas_call(
        body,
        name=name,
        in_specs=in_specs,
        out_shape=out_shapes,
        out_specs=out_specs or ([WHOLE] * len(out_shapes) if many else WHOLE),
        scratch_shapes=list(scratch),
        input_output_aliases=aliases or {},
        compiler_params=pltpu.CompilerParams(vmem_limit_bytes=28 * 1024 * 1024),
    )


def shape(dims, dtype):
    return jax.ShapeDtypeStruct(dims, dtype)


def tiles_to_line(block, first, count):
    return jnp.concatenate([block[first + j : first + j + 1] for j in range(count)], axis=1)


def line_to_tiles(ref, first, line):
    for j in range(line.shape[1] // LANES):
        ref[first + j : first + j + 1, :] = line[:, j * LANES : (j + 1) * LANES]


def tile_of(pair, tile):
    half = pair.shape[1] // LANES
    return pair[tile // half : tile // half + 1, (tile % half) * LANES : (tile % half + 1) * LANES]


def mode_of(pair, m, tiles):
    return jnp.concatenate([tile_of(pair, m * tiles + j) for j in range(tiles)], axis=1)


def lines_to_pair(lines):
    whole = jnp.concatenate(lines, axis=1)
    half = whole.shape[1] // 2
    return jnp.concatenate([whole[:, :half], whole[:, half:]], axis=0)


def upright(pair):
    count = 2 * pair.shape[1] // LANES
    block = jnp.concatenate([tile_of(pair, t) for t in range(count)] + [tile_of(pair, 0)] * (-count % 8), axis=0).T
    return jnp.concatenate([jnp.broadcast_to(block[:, t : t + 1], (LANES, LANES)) for t in range(count)], axis=0)


def two_terms(line):
    high = line.astype(BF16).astype(F32)
    row = lax.broadcasted_iota(jnp.int32, (16, line.shape[1]), 0)
    return jnp.where(row == 0, high, jnp.where(row == 1, line - high, 0.0)).astype(BF16)


def read_mode(ref, m, modes, owned, halves):
    per_owner = halves * modes * owned
    count = ref.shape[0] // per_owner
    parts = [
        jnp.concatenate(
            [ref[pl.ds((h * modes + m) * owned + i, count, stride=per_owner), :] for h in range(halves)], axis=1
        )
        for i in range(owned)
    ]
    return jnp.concatenate(parts, axis=0)


def score_body(modes, owned, rows_ref, protos_ref, kernel_ref, units_ref, unit_protos_ref, soft_ref, mass_ref, rows32):
    samples = units_ref.shape[0] // modes
    width = protos_ref.shape[0]
    halves = protos_ref.shape[1] // LANES
    raw = protos_ref[...].astype(F32)
    scale = lax.rsqrt(jnp.sum(raw * raw, axis=-1, keepdims=True) + 1e-6)
    unit_protos_ref[...] = (raw * scale).astype(BF16)
    rows32[...] = rows_ref[...].astype(F32)
    lines = []
    for m in range(modes):
        rows = slice(m * samples, (m + 1) * samples)
        raw = read_mode(rows32, m, modes, owned, halves)
        units = (raw * lax.rsqrt(jnp.sum(raw * raw, axis=-1, keepdims=True) + 1e-6)).astype(BF16)
        units_ref[rows, :] = units
        scores = lax.dot_general(units, unit_protos_ref[...], NT, preferred_element_type=F32)
        soft = jnp.exp2(scores * (10.0 * LOG2_E))
        kernel = soft * soft
        kernel_ref[rows, :] = kernel.astype(BF16)
        line_to_tiles(mass_ref, m * (width // LANES), jnp.sum(kernel, axis=0, keepdims=True))
        folded = soft[:, :LANES]
        for j in range(1, width // LANES):
            folded = folded + soft[:, j * LANES : (j + 1) * LANES]
        high = folded.astype(BF16)
        low = (folded - high.astype(F32)).astype(BF16)
        ones = jnp.ones((16, LANES), BF16)
        line = lax.dot_general(ones, high, NT, preferred_element_type=F32)
        line = line + lax.dot_general(ones, low, NT, preferred_element_type=F32)
        lines.append(line[0:1])
    soft_ref[...] = lines_to_pair(lines)


def row_body(modes, mass_ref, kernel_ref, *refs):
    samples = kernel_ref.shape[0] // modes
    tiles = kernel_ref.shape[1] // LANES
    inverse = 1.0 / mass_ref[...]
    lines = []
    for m in range(modes):
        terms = two_terms(tiles_to_line(inverse, m * tiles, tiles))
        kernel = kernel_ref[m * samples : (m + 1) * samples, :]
        line = lax.dot_general(terms, kernel, NT, preferred_element_type=F32)
        lines.append(line[0:1] + line[1:2])
    pair = lines_to_pair(lines)
    if len(refs) == 1:
        refs[0][...] = pair
    else:
        soft_ref, row_ref, inverse_ref = refs
        row_ref[...] = jnp.concatenate([pair, soft_ref[...]], axis=0)
        inverse_ref[...] = inverse


def column_body(modes, row_ref, kernel_ref, mass_ref):
    samples = kernel_ref.shape[0] // modes
    width = kernel_ref.shape[1]
    weight = 1.0 / row_ref[...]
    for m in range(modes):
        terms = two_terms(mode_of(weight, m, samples // LANES))
        kernel = kernel_ref[m * samples : (m + 1) * samples, :]
        line = jnp.dot(terms, kernel, preferred_element_type=F32)
        line_to_tiles(mass_ref, m * (width // LANES), line[0:1] + line[1:2])


def unit_body(modes, owned, place_ref, totals_ref, inverse_ref, units_ref, unit_protos_ref, tied_ref, *refs):
    pieces, (weights, sums) = refs[:-2], refs[-2:]
    samples = units_ref.shape[0] // modes
    width = unit_protos_ref.shape[0]
    tiles = width // LANES
    chunk = samples // owned // len(pieces)
    weights[0] = upright(COEFFICIENT / totals_ref[0:2])
    weights[1] = upright(2.0 * COEFFICIENT / totals_ref[2:4])
    step = 512
    for k in range(0, width, step):
        protos = unit_protos_ref[k : k + step, :]
        scores = lax.dot_general(units_ref[...], protos, NT, preferred_element_type=F32)
        codes, predicted = [], []
        for m in range(modes):
            rows = slice(m * samples, (m + 1) * samples)
            soft = jnp.exp2((10.0 * LOG2_E) * scores[rows])
            inverse = tiles_to_line(inverse_ref[...], m * tiles + k // LANES, step // LANES)
            codes.append(soft * soft * inverse * jnp.concatenate([weights[0, rows, :]] * (step // LANES), axis=1))
            predicted.append(soft * jnp.concatenate([weights[1, rows, :]] * (step // LANES), axis=1))
        for m in range(modes):
            rows = slice(m * samples, (m + 1) * samples)
            logit = predicted[m] - functools.reduce(jnp.add, [codes[n] for n in range(modes) if n != m])
            part = jnp.dot(logit.astype(BF16), protos, preferred_element_type=F32)
            sums[rows, :] = part if k == 0 else sums[rows, :] + part
    for step, piece in enumerate(pieces):
        place = lax.bitwise_xor(place_ref[0], jnp.int32(step)) * chunk
        for j in range(modes * owned):
            first = pl.multiple_of(place + j * (samples // owned), chunk)
            piece[j * chunk : (j + 1) * chunk, :] = sums[pl.ds(first, chunk), :].astype(BF16)


def proto_body(modes, totals_ref, inverse_ref, units_ref, unit_protos_ref, proto_ref):
    samples = units_ref.shape[0] // modes
    width = unit_protos_ref.shape[0]
    tiles = width // LANES
    inverse = inverse_ref[...].T
    weight = COEFFICIENT / totals_ref[0:2]
    spread = 2.0 * COEFFICIENT / totals_ref[2:4]
    weight = [mode_of(weight, m, samples // LANES) for m in range(modes)]
    spread = [mode_of(spread, m, samples // LANES) for m in range(modes)]
    step = 256
    for k in range(0, width, step):
        scores = lax.dot_general(unit_protos_ref[k : k + step, :], units_ref[...], NT, preferred_element_type=F32)
        codes, predicted = [], []
        for m in range(modes):
            first = m * tiles + k // LANES
            upright_inverse = jnp.concatenate([inverse[:, first + j : first + j + 1] for j in range(step // LANES)], axis=0)
            soft = jnp.exp2((10.0 * LOG2_E) * scores[:, m * samples : (m + 1) * samples])
            codes.append(soft * soft * upright_inverse * weight[m])
            predicted.append(soft * spread[m])
        logit = [
            (predicted[m] - functools.reduce(jnp.add, [codes[n] for n in range(modes) if n != m])).astype(BF16)
            for m in range(modes)
        ]
        proto_ref[k : k + step, :] = jnp.dot(
            jnp.concatenate(logit, axis=1), units_ref[...], preferred_element_type=F32
        ).astype(BF16)


def middle_body(place_ref, parts_ref, protos_ref, *refs):
    pieces, (grad_ref, rows_ref, unit) = refs[:-3], refs[-3:]
    total = jnp.sum(parts_ref[...].astype(F32), axis=0)
    share = total.shape[0]
    raw = protos_ref[pl.ds(pl.multiple_of(place_ref[0] * share, share), share), :].astype(F32)
    scale = lax.rsqrt(jnp.sum(raw * raw, axis=-1, keepdims=True) + 1e-6)
    inner = jnp.sum(total * raw, axis=-1, keepdims=True)
    grad_ref[...] = (scale * total - scale * scale * scale * inner * raw).astype(BF16)
    total = functools.reduce(jnp.add, [piece[...].astype(F32) for piece in pieces])
    for h in range(unit.shape[0]):
        unit[h] = total[:, h * LANES : (h + 1) * LANES]
    cuts = rows_ref.shape[0]
    for j in range(cuts):
        rows_ref[j] = jnp.concatenate(
            [unit[h, pl.ds(j, unit.shape[1] // cuts, stride=cuts), :] for h in range(unit.shape[0])], axis=0
        ).astype(BF16)


def last_body(parts_ref, raw_ref, protos_ref, grad_ref, proto_grad_ref):
    proto_grad_ref[...] = protos_ref[...].astype(F32)
    total = jnp.sum(parts_ref[...].astype(F32), axis=0)
    raw = raw_ref[...].astype(F32)
    count = raw.shape[0]
    total = jnp.concatenate([total[h : h + count] for h in range(0, total.shape[0], count)], axis=1)
    scale = lax.rsqrt(jnp.sum(raw * raw, axis=-1, keepdims=True) + 1e-6)
    inner = jnp.sum(total * raw, axis=-1, keepdims=True)
    grad = scale * total - scale * scale * scale * inner * raw
    modes, owned = grad_ref.shape[:2]
    for m in range(modes):
        grad_ref[m] = grad[m * owned : (m + 1) * owned]


def exchange(x, axes, order=None):
    return lax.all_to_all(x, axes, 0, 0, axis_index_groups=None if order is None else [order], tiled=True)


def copies(x, axes, count, order=None):
    return exchange(jnp.broadcast_to(x[None], (count,) + x.shape), axes, order)


def gather(x, axes, count, order=None):
    return copies(x, axes, count, order).reshape((count * x.shape[0],) + x.shape[1:])


def sum_over(x, axes, count, order=None):
    return jnp.sum(copies(x.astype(BF16), axes, count, order).astype(F32), axis=0)


def swap(x, axis, count, step):
    return lax.ppermute(x, axis, [(i, i ^ step) for i in range(count)]) if step else x


def per_device(sizes, embeddings, prototypes):
    modes, width = embeddings.shape[1:]
    own_samples = embeddings.shape[0]
    owned = own_samples * modes
    local_protos = prototypes.shape[0]
    ny, nc, nx, nz = (sizes[a] for a in ("y", "core", "x", "z"))
    dp = ("y", "core")
    groups = ny * nc
    lines = owned * nx * nz
    x_lines = lines // nx
    mass_shape = shape((modes * local_protos // LANES, LANES), F32)
    row_shape = shape((2, lines // 2), F32)
    units_shape = shape((lines, width), BF16)
    dp_place = lax.axis_index(dp).reshape(1)
    x_place = lax.axis_index("x").reshape(1)

    row_call = call(functools.partial(row_body, modes), "row_sum", row_shape, [WHOLE] * 2)
    last_row_call = call(
        functools.partial(row_body, modes), "row_sum", [shape((4, lines // 2), F32), mass_shape], [WHOLE] * 3
    )
    column_call = call(functools.partial(column_body, modes), "column_sum", mass_shape, [WHOLE] * 2)

    folded = list(range(0, nz, 2)) + list(range(1, nz, 2))[::-1]
    raw_rows = embeddings.transpose(1, 0, 2).reshape(owned, width)
    raw_tiles = jnp.concatenate([raw_rows[:, h : h + LANES] for h in range(0, width, LANES)], axis=0)
    gathered = gather(gather(raw_tiles, "z", nz, folded), "x", nx)
    kernel, units, unit_protos, soft, mass = call(
        functools.partial(score_body, modes, own_samples),
        "scores",
        [shape((lines, local_protos), BF16), units_shape, shape((local_protos, width), BF16), row_shape, mass_shape],
        [WHOLE] * 2,
        [pltpu.VMEM(gathered.shape, F32)],
    )(gathered, prototypes)

    for _ in range(2):
        row = row_call(sum_over(mass, ("core", "y"), groups), kernel)
        mass = column_call(sum_over(row, ("x", "z"), nx * nz, [x * nz + z for x in range(nx) for z in folded]), kernel)
    row, inverse = last_row_call(sum_over(mass, ("core", "y"), groups), kernel, soft)
    totals = sum_over(row, ("x", "z"), nx * nz, [x * nz + z for x in range(nx) for z in folded])

    proto_part = call(
        functools.partial(proto_body, modes), "proto_part", shape((local_protos, width), BF16), [WHOLE] * 4
    )(totals, inverse, units, unit_protos)
    pieces = call(
        functools.partial(unit_body, modes, own_samples),
        "unit_grad",
        [shape((x_lines, width), BF16)] * nx,
        [SCALARS] + [WHOLE] * 4 + [ANYWHERE],
        [pltpu.VMEM((2, lines, LANES), F32), pltpu.VMEM((lines, width), F32)],
    )(x_place, totals, inverse, units, unit_protos, proto_part)
    proto_part = exchange(proto_part, dp).reshape(groups, local_protos // groups, width)
    pieces = [pieces[0]] + [swap(pieces[step], "x", nx, step) for step in (2, 1, 3)]
    proto_grad, rows = call(
        middle_body,
        "middle",
        [shape((local_protos // groups, width), BF16), shape((nz, owned * width // LANES, LANES), BF16)],
        [SCALARS] + [WHOLE] * (2 + nx),
        [pltpu.VMEM((width // LANES, x_lines, LANES), F32)],
    )(dp_place, proto_part, prototypes, *pieces)
    rows = exchange(rows, "z", folded)
    proto_grad = lax.all_gather(proto_grad, dp, axis=0, tiled=True)
    embed_grad, proto_grad = call(
        last_body,
        "last",
        [shape((modes, own_samples, width), F32), shape((local_protos, width), F32)],
        [WHOLE] * 3,
    )(rows, raw_rows, proto_grad)
    return (embed_grad.transpose(1, 0, 2), proto_grad)


def solution(mesh):
    sizes = dict(y=mesh.shape["dp"] // 2, core=2, x=4, z=mesh.shape["proto"] // 4)
    fine = Mesh(mesh.devices.reshape(tuple(sizes.values())), tuple(sizes))
    specs = (P(("y", "core", "x", "z"), None, None), P(("x", "z"), None))
    return jax.shard_map(
        functools.partial(per_device, sizes), mesh=fine, in_specs=specs, out_specs=specs, check_vma=False
    )
```

```python
import functools

import jax
import jax.numpy as jnp
from jax import lax
from jax.experimental import pallas as pl
from jax.experimental.pallas import tpu as pltpu
from jax.sharding import Mesh, PartitionSpec as P

F32 = jnp.float32
BF16 = jnp.bfloat16
LANES = 128
COEFFICIENT = 64.0 * 10.0 / 6.0
LOG2_E = 1.4426950408889634
NT = (((1,), (1,)), ((), ()))
SCALARS = pl.BlockSpec(memory_space=pltpu.SMEM)
WHOLE = pl.BlockSpec(memory_space=pltpu.VMEM)
ANYWHERE = pl.BlockSpec(memory_space=pl.ANY)


def call(body, name, out_shapes, in_specs, scratch=(), out_specs=None, aliases=None):
    many = isinstance(out_shapes, (list, tuple))
    return pl.pallas_call(
        body,
        name=name,
        in_specs=in_specs,
        out_shape=out_shapes,
        out_specs=out_specs or ([WHOLE] * len(out_shapes) if many else WHOLE),
        scratch_shapes=list(scratch),
        input_output_aliases=aliases or {},
        compiler_params=pltpu.CompilerParams(vmem_limit_bytes=28 * 1024 * 1024),
    )


def shape(dims, dtype):
    return jax.ShapeDtypeStruct(dims, dtype)


def tiles_to_line(block, first, count):
    return jnp.concatenate([block[first + j : first + j + 1] for j in range(count)], axis=1)


def line_to_tiles(ref, first, line):
    for j in range(line.shape[1] // LANES):
        ref[first + j : first + j + 1, :] = line[:, j * LANES : (j + 1) * LANES]


def tile_of(pair, tile):
    half = pair.shape[1] // LANES
    return pair[tile // half : tile // half + 1, (tile % half) * LANES : (tile % half + 1) * LANES]


def mode_of(pair, m, tiles):
    return jnp.concatenate([tile_of(pair, m * tiles + j) for j in range(tiles)], axis=1)


def lines_to_pair(lines):
    whole = jnp.concatenate(lines, axis=1)
    half = whole.shape[1] // 2
    return jnp.concatenate([whole[:, :half], whole[:, half:]], axis=0)


def upright(pair):
    count = 2 * pair.shape[1] // LANES
    block = jnp.concatenate([tile_of(pair, t) for t in range(count)] + [tile_of(pair, 0)] * (-count % 8), axis=0).T
    return jnp.concatenate([jnp.broadcast_to(block[:, t : t + 1], (LANES, LANES)) for t in range(count)], axis=0)


def two_terms(line):
    high = line.astype(BF16).astype(F32)
    row = lax.broadcasted_iota(jnp.int32, (16, line.shape[1]), 0)
    return jnp.where(row == 0, high, jnp.where(row == 1, line - high, 0.0)).astype(BF16)


def read_mode(ref, m, modes, owned, halves):
    per_owner = halves * modes * owned
    count = ref.shape[0] // per_owner
    parts = [
        jnp.concatenate(
            [ref[pl.ds((h * modes + m) * owned + i, count, stride=per_owner), :] for h in range(halves)], axis=1
        )
        for i in range(owned)
    ]
    return jnp.concatenate(parts, axis=0)


def score_body(modes, owned, rows_ref, protos_ref, kernel_ref, units_ref, unit_protos_ref, soft_ref, mass_ref, rows32):
    samples = units_ref.shape[0] // modes
    width = protos_ref.shape[0]
    halves = protos_ref.shape[1] // LANES
    raw = protos_ref[...].astype(F32)
    scale = lax.rsqrt(jnp.sum(raw * raw, axis=-1, keepdims=True) + 1e-6)
    unit_protos_ref[...] = (raw * scale).astype(BF16)
    rows32[...] = rows_ref[...].astype(F32)
    lines = []
    for m in range(modes):
        rows = slice(m * samples, (m + 1) * samples)
        raw = read_mode(rows32, m, modes, owned, halves)
        units = (raw * lax.rsqrt(jnp.sum(raw * raw, axis=-1, keepdims=True) + 1e-6)).astype(BF16)
        units_ref[rows, :] = units
        scores = lax.dot_general(units, unit_protos_ref[...], NT, preferred_element_type=F32)
        soft = jnp.exp2(scores * (10.0 * LOG2_E))
        kernel = soft * soft
        kernel_ref[rows, :] = kernel.astype(BF16)
        line_to_tiles(mass_ref, m * (width // LANES), jnp.sum(kernel, axis=0, keepdims=True))
        folded = soft[:, :LANES]
        for j in range(1, width // LANES):
            folded = folded + soft[:, j * LANES : (j + 1) * LANES]
        high = folded.astype(BF16)
        low = (folded - high.astype(F32)).astype(BF16)
        ones = jnp.ones((16, LANES), BF16)
        line = lax.dot_general(ones, high, NT, preferred_element_type=F32)
        line = line + lax.dot_general(ones, low, NT, preferred_element_type=F32)
        lines.append(line[0:1])
    soft_ref[...] = lines_to_pair(lines)


def row_body(modes, mass_ref, kernel_ref, *refs):
    samples = kernel_ref.shape[0] // modes
    tiles = kernel_ref.shape[1] // LANES
    inverse = 1.0 / mass_ref[...]
    lines = []
    for m in range(modes):
        terms = two_terms(tiles_to_line(inverse, m * tiles, tiles))
        kernel = kernel_ref[m * samples : (m + 1) * samples, :]
        line = lax.dot_general(terms, kernel, NT, preferred_element_type=F32)
        lines.append(line[0:1] + line[1:2])
    pair = lines_to_pair(lines)
    if len(refs) == 1:
        refs[0][...] = pair
    else:
        soft_ref, row_ref, inverse_ref = refs
        row_ref[...] = jnp.concatenate([pair, soft_ref[...]], axis=0)
        inverse_ref[...] = inverse


def column_body(modes, row_ref, kernel_ref, mass_ref):
    samples = kernel_ref.shape[0] // modes
    width = kernel_ref.shape[1]
    weight = 1.0 / row_ref[...]
    for m in range(modes):
        terms = two_terms(mode_of(weight, m, samples // LANES))
        kernel = kernel_ref[m * samples : (m + 1) * samples, :]
        line = jnp.dot(terms, kernel, preferred_element_type=F32)
        line_to_tiles(mass_ref, m * (width // LANES), line[0:1] + line[1:2])


def unit_body(modes, owned, place_ref, totals_ref, inverse_ref, units_ref, unit_protos_ref, tied_ref, *refs):
    pieces, (weights, sums) = refs[:-2], refs[-2:]
    samples = units_ref.shape[0] // modes
    width = unit_protos_ref.shape[0]
    tiles = width // LANES
    chunk = samples // owned // len(pieces)
    weights[0] = upright(COEFFICIENT / totals_ref[0:2])
    weights[1] = upright(2.0 * COEFFICIENT / totals_ref[2:4])
    step = 512
    for k in range(0, width, step):
        protos = unit_protos_ref[k : k + step, :]
        scores = lax.dot_general(units_ref[...], protos, NT, preferred_element_type=F32)
        codes, predicted = [], []
        for m in range(modes):
            rows = slice(m * samples, (m + 1) * samples)
            soft = jnp.exp2((10.0 * LOG2_E) * scores[rows])
            inverse = tiles_to_line(inverse_ref[...], m * tiles + k // LANES, step // LANES)
            codes.append(soft * soft * inverse * jnp.concatenate([weights[0, rows, :]] * (step // LANES), axis=1))
            predicted.append(soft * jnp.concatenate([weights[1, rows, :]] * (step // LANES), axis=1))
        for m in range(modes):
            rows = slice(m * samples, (m + 1) * samples)
            logit = predicted[m] - functools.reduce(jnp.add, [codes[n] for n in range(modes) if n != m])
            part = jnp.dot(logit.astype(BF16), protos, preferred_element_type=F32)
            sums[rows, :] = part if k == 0 else sums[rows, :] + part
    for step, piece in enumerate(pieces):
        place = lax.bitwise_xor(place_ref[0], jnp.int32(step)) * chunk
        for j in range(modes * owned):
            first = pl.multiple_of(place + j * (samples // owned), chunk)
            piece[j * chunk : (j + 1) * chunk, :] = sums[pl.ds(first, chunk), :].astype(BF16)


def proto_body(modes, totals_ref, inverse_ref, units_ref, unit_protos_ref, kernel_ref, proto_ref):
    samples = units_ref.shape[0] // modes
    width = unit_protos_ref.shape[0]
    tiles = width // LANES
    copies_across = units_ref.shape[1] // LANES
    rows = [slice(m * samples, (m + 1) * samples) for m in range(modes)]
    weight = jnp.concatenate([upright(COEFFICIENT / totals_ref[0:2])] * copies_across, axis=1)
    spread = jnp.concatenate([upright(2.0 * COEFFICIENT / totals_ref[2:4])] * copies_across, axis=1)
    units = [units_ref[rows[m], :].astype(F32) for m in range(modes)]
    for_predicted = jnp.concatenate([(spread[rows[m]] * units[m]).astype(BF16) for m in range(modes)], axis=0)
    for_codes = [
        (weight[rows[m]] * functools.reduce(jnp.add, [units[n] for n in range(modes) if n != m])).T.astype(BF16)
        for m in range(modes)
    ]
    step = 256
    for k in range(0, width, step):
        scores = lax.dot_general(unit_protos_ref[k : k + step, :], units_ref[...], NT, preferred_element_type=F32)
        soft = jnp.exp2((10.0 * LOG2_E) * scores).astype(BF16)
        total = jnp.dot(soft, for_predicted, preferred_element_type=F32)
        codes = jnp.zeros((units_ref.shape[1], step), F32)
        for m in range(modes):
            inverse = tiles_to_line(inverse_ref[...], m * tiles + k // LANES, step // LANES)
            codes = codes + inverse * jnp.dot(for_codes[m], kernel_ref[rows[m], k : k + step], preferred_element_type=F32)
        proto_ref[k : k + step, :] = (total - codes.T).astype(BF16)


def middle_body(place_ref, parts_ref, protos_ref, *refs):
    pieces, (grad_ref, rows_ref, unit) = refs[:-3], refs[-3:]
    total = jnp.sum(parts_ref[...].astype(F32), axis=0)
    share = total.shape[0]
    raw = protos_ref[pl.ds(pl.multiple_of(place_ref[0] * share, share), share), :].astype(F32)
    scale = lax.rsqrt(jnp.sum(raw * raw, axis=-1, keepdims=True) + 1e-6)
    inner = jnp.sum(total * raw, axis=-1, keepdims=True)
    grad_ref[...] = (scale * total - scale * scale * scale * inner * raw).astype(BF16)
    total = functools.reduce(jnp.add, [piece[...].astype(F32) for piece in pieces])
    for h in range(unit.shape[0]):
        unit[h] = total[:, h * LANES : (h + 1) * LANES]
    cuts = rows_ref.shape[0]
    for j in range(cuts):
        rows_ref[j] = jnp.concatenate(
            [unit[h, pl.ds(j, unit.shape[1] // cuts, stride=cuts), :] for h in range(unit.shape[0])], axis=0
        ).astype(BF16)


def last_body(parts_ref, raw_ref, protos_ref, grad_ref, proto_grad_ref):
    proto_grad_ref[...] = protos_ref[...].astype(F32)
    total = jnp.sum(parts_ref[...].astype(F32), axis=0)
    raw = raw_ref[...].astype(F32)
    count = raw.shape[0]
    total = jnp.concatenate([total[h : h + count] for h in range(0, total.shape[0], count)], axis=1)
    scale = lax.rsqrt(jnp.sum(raw * raw, axis=-1, keepdims=True) + 1e-6)
    inner = jnp.sum(total * raw, axis=-1, keepdims=True)
    grad = scale * total - scale * scale * scale * inner * raw
    modes, owned = grad_ref.shape[:2]
    for m in range(modes):
        grad_ref[m] = grad[m * owned : (m + 1) * owned]


def exchange(x, axes):
    return lax.all_to_all(x, axes, 0, 0, tiled=True)


def copies(x, axes, count):
    return exchange(jnp.broadcast_to(x[None], (count,) + x.shape), axes)


def gather(x, axes, count):
    return copies(x, axes, count).reshape((count * x.shape[0],) + x.shape[1:])


def sum_over(x, axes, count):
    return jnp.sum(copies(x.astype(BF16), axes, count).astype(F32), axis=0)


def swap(x, axis, count, step):
    return lax.ppermute(x, axis, [(i, i ^ step) for i in range(count)]) if step else x


def per_device(sizes, embeddings, prototypes):
    modes, width = embeddings.shape[1:]
    own_samples = embeddings.shape[0]
    owned = own_samples * modes
    local_protos = prototypes.shape[0]
    ny, nc, nx, nz = (sizes[a] for a in ("y", "core", "x", "z"))
    dp = ("y", "core")
    groups = ny * nc
    lines = owned * nx * nz
    x_lines = lines // nx
    mass_shape = shape((modes * local_protos // LANES, LANES), F32)
    row_shape = shape((2, lines // 2), F32)
    units_shape = shape((lines, width), BF16)
    dp_place = lax.axis_index(dp).reshape(1)
    x_place = lax.axis_index("x").reshape(1)

    row_call = call(functools.partial(row_body, modes), "row_sum", row_shape, [WHOLE] * 2)
    last_row_call = call(
        functools.partial(row_body, modes), "row_sum", [shape((4, lines // 2), F32), mass_shape], [WHOLE] * 3
    )
    column_call = call(functools.partial(column_body, modes), "column_sum", mass_shape, [WHOLE] * 2)

    raw_rows = embeddings.transpose(1, 0, 2).reshape(owned, width)
    raw_tiles = jnp.concatenate([raw_rows[:, h : h + LANES] for h in range(0, width, LANES)], axis=0)
    gathered = gather(gather(raw_tiles, "z", nz), "x", nx)
    kernel, units, unit_protos, soft, mass = call(
        functools.partial(score_body, modes, own_samples),
        "scores",
        [shape((lines, local_protos), BF16), units_shape, shape((local_protos, width), BF16), row_shape, mass_shape],
        [WHOLE] * 2,
        [pltpu.VMEM(gathered.shape, F32)],
    )(gathered, prototypes)

    for _ in range(2):
        row = row_call(sum_over(mass, ("core", "y"), groups), kernel)
        mass = column_call(sum_over(row, ("x", "z"), nx * nz), kernel)
    row, inverse = last_row_call(sum_over(mass, ("core", "y"), groups), kernel, soft)
    totals = sum_over(row, ("x", "z"), nx * nz)

    proto_part = call(
        functools.partial(proto_body, modes), "proto_part", shape((local_protos, width), BF16), [WHOLE] * 5
    )(totals, inverse, units, unit_protos, kernel)
    pieces = call(
        functools.partial(unit_body, modes, own_samples),
        "unit_grad",
        [shape((x_lines, width), BF16)] * nx,
        [SCALARS] + [WHOLE] * 4 + [ANYWHERE],
        [pltpu.VMEM((2, lines, LANES), F32), pltpu.VMEM((lines, width), F32)],
    )(x_place, totals, inverse, units, unit_protos, proto_part)
    proto_part = exchange(proto_part, dp).reshape(groups, local_protos // groups, width)
    pieces = [pieces[0]] + [swap(pieces[step], "x", nx, step) for step in (2, 1, 3)]
    proto_grad, rows = call(
        middle_body,
        "middle",
        [shape((local_protos // groups, width), BF16), shape((nz, owned * width // LANES, LANES), BF16)],
        [SCALARS] + [WHOLE] * (2 + nx),
        [pltpu.VMEM((width // LANES, x_lines, LANES), F32)],
    )(dp_place, proto_part, prototypes, *pieces)
    rows = exchange(rows, "z")
    proto_grad = lax.all_gather(proto_grad, dp, axis=0, tiled=True)
    embed_grad, proto_grad = call(
        last_body,
        "last",
        [shape((modes, own_samples, width), F32), shape((local_protos, width), F32)],
        [WHOLE] * 3,
    )(rows, raw_rows, proto_grad)
    return (embed_grad.transpose(1, 0, 2), proto_grad)


def solution(mesh):
    sizes = dict(y=mesh.shape["dp"] // 2, core=2, x=4, z=mesh.shape["proto"] // 4)
    fine = Mesh(mesh.devices.reshape(tuple(sizes.values())), tuple(sizes))
    specs = (P(("y", "core", "x", "z"), None, None), P(("x", "z"), None))
    return jax.shard_map(
        functools.partial(per_device, sizes), mesh=fine, in_specs=specs, out_specs=specs, check_vma=False
    )
```
